32 devices in a mesh: slab: 8 (over z, x), quad: 4 (over y, core).
Axes of the slice: x: 2, y: 2, z: 4, core: 2. Of those that a mesh axis runs over, the one named last changes fastest.
Arguments:
- right_side: float32 [32, 64, 1024], P('slab', 'quad'), may hold values from -16 to 16
- phase_label: int32 [32, 64, 1024], P('slab', 'quad'), may hold values 0 or 1
- density_gain: float32 [32, 64, 1024], P('slab', 'quad'), may hold values from 0.25 to 1.75
- subdomain: int32 [32, 64, 1024], P('slab', 'quad'), may hold values from 0 to 63, as said below
- block_factor: float32 [8, 256, 256], P('slab', 'quad'), may hold values from -0.03125 to 0.03125
- coupling: float32 [8, 256, 64], P('slab', 'quad'), may hold values from -0.75 to 0.75
Outputs:
- solution_field: float32 [32, 64, 1024], P('slab', 'quad')
- residual: float32 [32, 64, 1024], P('slab', 'quad')
The draws below stay inside these ranges and needn't reach their ends.
Inputs may be any that keep to these rules, and one draw needn't show every extreme that they name: `subdomain`: within each device the subdomains are 8 x 8 contiguous tiles with jagged edges, each spanning the device's z-planes.
All inputs are finite; a program needn't handle non-finite values. No bound on the sum of `phase_label` on one device may be relied on, other than what follows from the above.
Results may differ from the reference program's by a relative error of at most 0.0075.
Values sent between devices are 32-bit elements; how exact they have to be, the bound alone decides.
A program may use at most 64 MiB of HBM per device.

```python
import jax
import jax.numpy as jnp
from jax import lax

CZ = 4
CY = 16
NX = 1024
LINE = 4
SUB_Y = 8
SUB_X = 8
ITERS = 2
SUBS = 64
COARSE = 256
SLABS = 8
NZ = 32
NY = 64
N_QUAD = 4


def draw_subdomain(key, part):
    keyed = jax.random.fold_in(key, 11)
    key_y, key_x = jax.random.split(keyed)
    jitter_y = jax.random.randint(key_y, (NZ, 1, NX), 0, CY // 2 + 1)
    jitter_x = jax.random.randint(key_x, (NZ, NY, 1), 0, NX // 2 + 1)
    ypos = lax.broadcasted_iota(jnp.int32, (NZ, NY, NX), 1) % CY
    xpos = lax.broadcasted_iota(jnp.int32, (NZ, NY, NX), 2)
    tile_y = jnp.minimum((ypos * SUB_Y + jitter_y) // CY, SUB_Y - 1)
    tile_x = jnp.minimum((xpos * SUB_X + jitter_x) // NX, SUB_X - 1)
    return (tile_y * SUB_X + tile_x).astype(jnp.int32)


def draw_right_side(key, part):
    keyed = jax.random.fold_in(key, 23)
    zpos = lax.broadcasted_iota(jnp.float32, (NZ, NY, NX), 0)
    rising = jnp.exp(jnp.log(3.0) * zpos / max(NZ - 1, 1))
    values = jax.random.truncated_normal(keyed, -5.0, 5.0, (NZ, NY, NX), jnp.float32) * rising
    return values.astype(jnp.float32)


def set_ends(array, own_key, least, top_value):
    shape = array.shape
    spot = [jax.random.randint(jax.random.fold_in(own_key, axis), (), 0, shape[axis]) for axis in range(len(shape))]
    array = array.at[tuple(spot)].set(least)
    longest = shape.index(max(shape))
    spot[longest] = (spot[longest] + 1) % shape[longest]
    return array.at[tuple(spot)].set(top_value)


def level_of(rng, dims, cuts, least, top_value):
    def one(axis_at, parts):
        heights = jax.random.uniform(jax.random.fold_in(jax.random.fold_in(rng, 6), axis_at), (parts,), jnp.float32, least / len(cuts), top_value / len(cuts))
        return jnp.repeat(jnp.exp(heights), dims[axis_at] // parts).reshape((-1,) + (1,) * (len(dims) - axis_at - 1))

    factor_of = one(*cuts[0])
    for cut in cuts[1:]:
        factor_of = factor_of * one(*cut)
    return factor_of


def normal_values(rng, shape, width, reach, cuts=(), dtype=jnp.bfloat16):
    result = width * jax.random.normal(rng, shape, jnp.float32)
    if cuts:
        result = result * level_of(rng, shape, cuts, -0.22, 0.18)
    return jnp.clip(result, -reach, reach).astype(dtype)


def setup_inputs(seed: int = 0) -> dict:
    key_of = jax.random.split(jax.random.key(seed), 7)
    return {
        "right_side": draw_right_side(jax.random.fold_in(key_of[6], 71), 0),
        "phase_label": set_ends((jax.random.randint(key_of[1], (NZ, NY, NX), 0, 4) < 3).astype(jnp.int32), jax.random.fold_in(key_of[1], 1), 0, 1),
        "density_gain": jnp.clip(1.0 + 0.15 * jax.random.normal(key_of[2], (NZ, NY, NX), jnp.float32), 0.25, 1.75),
        "subdomain": draw_subdomain(jax.random.fold_in(key_of[6], 71), 0),
        "block_factor": normal_values(key_of[4], (SLABS, COARSE, COARSE), (0.5 / COARSE), 0.03125, ((0, 8), (1, 4)), jnp.float32),
        "coupling": normal_values(key_of[5], (SLABS, COARSE, SUBS), (1.1 * SUBS) ** -0.5, 0.75, ((0, 8), (1, 4)), jnp.float32),
    }


HIGH = lax.Precision.HIGHEST


def harmonic(here, there):
    return jnp.where(there > 0, 2.0 * here * there / (here + there), here)


def solve_along_line(diag, lower, upper, rhs):
    shape = rhs.shape
    dd = diag.reshape(-1, LINE, shape[1], shape[2])
    lo = lower.reshape(-1, LINE, shape[1], shape[2])
    up = upper.reshape(-1, LINE, shape[1], shape[2])
    rr = rhs.reshape(-1, LINE, shape[1], shape[2])
    gammas = []
    rhos = []
    denom = dd[:, 0]
    gammas.append(-up[:, 0] / denom)
    rhos.append(rr[:, 0] / denom)
    for j in range(1, LINE):
        denom = dd[:, j] + lo[:, j] * gammas[j - 1]
        gammas.append(-up[:, j] / denom)
        rhos.append((rr[:, j] + lo[:, j] * rhos[j - 1]) / denom)
    values = [None] * LINE
    values[LINE - 1] = rhos[LINE - 1]
    for j in range(LINE - 2, -1, -1):
        values[j] = rhos[j] - gammas[j] * values[j + 1]
    return jnp.stack(values, axis=1).reshape(shape)


def reference(right_side, phase_label, density_gain, subdomain, block_factor, coupling):
    mobility = 1.0 / (density_gain * (0.001 + 0.999 * phase_label.astype(jnp.float32)))
    mpad = jnp.pad(mobility, 1)
    kz_lo = harmonic(mobility, mpad[:-2, 1:-1, 1:-1])
    kz_hi = harmonic(mobility, mpad[2:, 1:-1, 1:-1])
    ky_lo = harmonic(mobility, mpad[1:-1, :-2, 1:-1])
    ky_hi = harmonic(mobility, mpad[1:-1, 2:, 1:-1])
    kx_lo = harmonic(mobility, mpad[1:-1, 1:-1, :-2])
    kx_hi = harmonic(mobility, mpad[1:-1, 1:-1, 2:])
    diag = kz_lo + kz_hi + ky_lo + ky_hi + kx_lo + kx_hi

    def apply_a(field):
        vp = jnp.pad(field, 1)
        return (diag * field - kz_lo * vp[:-2, 1:-1, 1:-1] - kz_hi * vp[2:, 1:-1, 1:-1]
                - ky_lo * vp[1:-1, :-2, 1:-1] - ky_hi * vp[1:-1, 2:, 1:-1]
                - kx_lo * vp[1:-1, 1:-1, :-2] - kx_hi * vp[1:-1, 1:-1, 2:])

    zpos = lax.broadcasted_iota(jnp.int32, right_side.shape, 0)
    ypos = lax.broadcasted_iota(jnp.int32, right_side.shape, 1)
    global_id = ((zpos // CZ) * COARSE + (ypos // CY) * SUBS + subdomain).astype(jnp.int32)
    flat_id = global_id.reshape(-1)
    mats = coupling.reshape(SLABS, N_QUAD, SUBS, SUBS)

    def precondition(resid):
        block_part = solve_along_line(diag, kz_lo, kz_hi, resid)
        coarse_in = jax.ops.segment_sum(resid.reshape(-1), flat_id, num_segments=SLABS * COARSE).reshape(SLABS, COARSE)
        coarse_rhs = jnp.einsum("kij,kj->ki", block_factor, coarse_in, precision=HIGH).reshape(SLABS, N_QUAD, SUBS)

        def upward(prev, pair):
            mat, vec = pair
            now = jnp.einsum("qij,qj->qi", mat, prev, precision=HIGH) + vec
            return now, now

        start = jnp.zeros((N_QUAD, SUBS), jnp.float32)
        unused, u_all = lax.scan(upward, start, (mats, coarse_rhs))

        def downward(s_next, pair):
            mat, uval = pair
            wval = uval + s_next
            return jnp.einsum("qji,qj->qi", mat, wval, precision=HIGH), wval

        unused2, w_all = lax.scan(downward, start, (mats, u_all), reverse=True)
        coarse_out = jnp.einsum("kji,kj->ki", block_factor, w_all.reshape(SLABS, COARSE), precision=HIGH)
        return block_part + coarse_out.reshape(-1)[flat_id].reshape(resid.shape)

    solution_field = jnp.zeros_like(right_side)
    residual = right_side
    precond = precondition(residual)
    search_direction = precond
    rz = jnp.sum(residual * precond)
    for step in range(ITERS):
        image = apply_a(search_direction)
        alpha = rz / jnp.sum(search_direction * image)
        solution_field = solution_field + alpha * search_direction
        residual = residual - alpha * image
        if step + 1 < ITERS:
            precond = precondition(residual)
            residual_precond_next = jnp.sum(residual * precond)
            search_direction = precond + (residual_precond_next / rz) * search_direction
            rz = residual_precond_next
    return solution_field, residual
```

```python
import functools

import jax
import jax.numpy as jnp
from jax import lax
from jax.experimental import pallas as pl
from jax.experimental.pallas import tpu as pltpu
from jax.sharding import PartitionSpec as P

LINE = 4
ITERS = 2
MESH = pl.DeviceIdType.MESH
F32 = jnp.float32
BF16 = jnp.bfloat16


def kernel(ns, nq, b_ref, phase_ref, gain_ref, sub_ref, fac_ref, cpl_ref, x_ref, r_ref,
           kz, kyl, kyh, kxl, kxh, diag, inv, gam, hot_hi, hot_lo, p0, q0, bj, zz,
           cg, qbuf, sbuf, rbuf, dbuf, ebuf, fbuf, zhalo, yhalo, ysend,
           cg_ss, cg_rs, q_ss, q_rs, s_ss, s_rs, r_ss, r_rs, d_ss, d_rs, e_ss, e_rs, f_ss, f_rs, h_ss, h_rs):
    k = lax.axis_index("slab")
    q = lax.axis_index("quad")
    cz, cy, nx = b_ref.shape
    count = cpl_ref.shape[2]
    pending = []

    barrier = pltpu.get_barrier_semaphore()
    for d in range(1, ns):
        pl.semaphore_signal(barrier, inc=1, device_id={"slab": lax.rem(k + d, ns)}, device_id_type=MESH)
    for d in range(1, nq):
        pl.semaphore_signal(barrier, inc=1, device_id={"quad": lax.rem(q + d, nq)}, device_id_type=MESH)

    def copies(axis, me, n, buf, ss, rs):
        out = []
        for d in range(1, n):
            out.append(pltpu.make_async_remote_copy(
                src_ref=buf.at[me], dst_ref=buf.at[me], send_sem=ss.at[d], recv_sem=rs.at[d],
                device_id={axis: lax.rem(me + d, n)}, device_id_type=MESH))
        return out

    def gather_start(axis, me, n, buf, ss, rs):
        for c in copies(axis, me, n, buf, ss, rs):
            c.start()
            pending.append(c)

    def gather_wait(axis, me, n, buf, ss, rs):
        for d in range(1, n):
            at = lax.rem(me + n - d, n)
            pltpu.make_async_remote_copy(
                src_ref=buf.at[at], dst_ref=buf.at[at], send_sem=ss.at[d], recv_sem=rs.at[d],
                device_id={axis: at}, device_id_type=MESH).wait_recv()

    row = lax.broadcasted_iota(jnp.int32, (cy, nx), 0)
    lane = lax.broadcasted_iota(jnp.int32, (cy, nx), 1)
    sub8 = lax.broadcasted_iota(jnp.int32, (8, 128), 0)
    lane8 = lax.broadcasted_iota(jnp.int32, (8, 128), 1)
    eye = (lax.broadcasted_iota(jnp.int32, (count, count), 0)
           == lax.broadcasted_iota(jnp.int32, (count, count), 1)).astype(F32)

    def halo_parts(slot, src):
        up, down = jnp.minimum(k + 1, ns - 1), jnp.maximum(k - 1, 0)
        right, left = jnp.minimum(q + 1, nq - 1), jnp.maximum(q - 1, 0)

        def copy(s, dst, i, axis, to):
            return pltpu.make_async_remote_copy(
                src_ref=s, dst_ref=dst, send_sem=h_ss.at[slot, i], recv_sem=h_rs.at[slot, i],
                device_id={axis: to}, device_id_type=MESH)

        return (
            (k < ns - 1, k > 0, copy(src.at[cz - 1], zhalo.at[slot, 0], 0, "slab", up)),
            (k > 0, k < ns - 1, copy(src.at[0], zhalo.at[slot, 1], 1, "slab", down)),
            (q < nq - 1, q > 0, copy(ysend.at[slot, 1], yhalo.at[slot, 0], 2, "quad", right)),
            (q > 0, q < nq - 1, copy(ysend.at[slot, 0], yhalo.at[slot, 1], 3, "quad", left)),
        )

    def halo_clear(slot):
        for buf, i, edge in ((zhalo, 0, k == 0), (zhalo, 1, k == ns - 1),
                             (yhalo, 0, q == 0), (yhalo, 1, q == nq - 1)):
            @pl.when(edge)
            def _(buf=buf, i=i):
                buf[slot, i] = jnp.zeros(buf.shape[2:], F32)

    def halo_start(slot, src):
        for j in range(cz):
            ysend[slot, 0, j:j + 1] = src[j, 0:1]
            ysend[slot, 1, j:j + 1] = src[j, cy - 1:cy]
        for sends, unused, c in halo_parts(slot, src):
            @pl.when(sends)
            def _(c=c):
                c.start()

    def halo_wait(slot, src):
        for sends, receives, c in halo_parts(slot, src):
            @pl.when(receives)
            def _(c=c):
                c.wait_recv()

            @pl.when(sends)
            def _(c=c):
                c.wait_send()

    def y_below(slot, plane, j):
        return jnp.where(row == 0, yhalo[slot, 0, j:j + 1], pltpu.roll(plane, 1, 0))

    def y_above(slot, plane, j):
        return jnp.where(row == cy - 1, yhalo[slot, 1, j:j + 1], pltpu.roll(plane, cy - 1, 0))

    def harmonic(here, there):
        return jnp.where(there > 0, 2.0 * here * there / (here + there), here)

    def restrict(planes):
        total = None
        for j in range(cz):
            high = planes[j].astype(BF16)
            low = (planes[j] - high.astype(F32)).astype(BF16)
            lhs = jnp.concatenate([part * hot_hi[j, h] for part in (high, low) for h in range(8)], axis=0)
            now = lax.dot_general(lhs, hot_lo[j], (((1,), (1,)), ((), ())), preferred_element_type=F32)
            total = now if total is None else total + now
        total = total[:8 * cy] + total[8 * cy:]
        spot = lax.broadcasted_iota(jnp.int32, total.shape, 0) % cy
        across = lax.broadcasted_iota(jnp.int32, total.shape, 1) // 8
        total = jnp.where(spot == across, total, 0.0)
        tile = jnp.concatenate(
            [jnp.sum(total[cy * h:cy * (h + 1)], axis=0, keepdims=True) for h in range(8)], axis=0)
        for shift in (8, 16, 32, 64):
            tile = tile + pltpu.roll(tile, shift, 1)
        return jnp.sum(jnp.where(sub8 == lane8 // 8, tile, 0.0), axis=0, keepdims=True)

    def partial(left, right):
        total = left[0] * right[0]
        for j in range(1, cz):
            total = total + left[j] * right[j]
        total = total[:8] + total[8:]
        tile = total[:, :128]
        for c in range(1, nx // 128):
            tile = tile + total[:, 128 * c:128 * (c + 1)]
        return jnp.sum(tile, axis=0, keepdims=True)

    def solve_lines(planes):
        rho = [planes[0] * inv[0]]
        for j in range(1, LINE):
            rho.append((planes[j] + kz[j] * rho[j - 1]) * inv[j])
        values = [None] * LINE
        values[LINE - 1] = rho[LINE - 1]
        for j in range(LINE - 2, -1, -1):
            values[j] = rho[j] - gam[j] * values[j + 1]
        return values

    def message(first, second):
        return jnp.where(sub8 == 0, first, second)

    def coarse_rhs(slot):
        rows = [qbuf[slot, i, 0:1] for i in range(nq)]
        pieces = [rows[2 * i] + pltpu.roll(rows[2 * i + 1], 64, 1) for i in range(nq // 2)]
        whole = jnp.concatenate(pieces, axis=1)
        column = jnp.sum(fac_ref[0] * whole, axis=1, keepdims=True)
        return jnp.sum(jnp.concatenate([eye, jnp.zeros_like(eye)], axis=1) * column, axis=0, keepdims=True)

    def chain(rhs):
        us = [rhs[0][:, :count]]
        sq_row, sq_col = us[0] * us[0], None
        for i in range(1, ns):
            if i % 2:
                now = jnp.sum(cg[i] * us[i - 1] + eye * rhs[i][:, :count], axis=1, keepdims=True)
                sq_col = now * now if sq_col is None else sq_col + now * now
            else:
                now = jnp.sum(cg[i] * us[i - 1], axis=0, keepdims=True) + rhs[i][:, :count]
                sq_row = sq_row + now * now
            us.append(now)
        w = us[ns - 1]
        own_row = jnp.zeros((1, count), F32)
        own_col = jnp.where(k == ns - 1, w, 0.0)
        for i in range(ns - 1, 0, -1):
            if i % 2:
                w = jnp.sum(cg[i] * w, axis=0, keepdims=True) + us[i - 1]
                own_row = jnp.where(k == i - 1, w, own_row)
            else:
                w = jnp.sum(cg[i] * w, axis=1, keepdims=True) + us[i - 1]
                own_col = jnp.where(k == i - 1, w, own_col)
        own = own_col + jnp.sum(eye * own_row, axis=1, keepdims=True)
        square = jnp.sum(sq_row, axis=1, keepdims=True) + jnp.sum(sq_col, axis=0, keepdims=True)
        share = jnp.sum(fac_ref[0] * own, axis=0, keepdims=True)
        return share, square

    def interpolate(table, j):
        wide = jnp.broadcast_to(table, (cy, 128))
        return jnp.concatenate(
            [jnp.take_along_axis(wide, sub_ref[j, :, 128 * c:128 * (c + 1)], axis=1, mode="promise_in_bounds")
             for c in range(nx // 128)], axis=1)

    def own_table(slot):
        total = rbuf[slot, 0]
        for i in range(1, nq):
            total = total + rbuf[slot, i]
        table = total[0:1, :128]
        for i in range(1, nq // 2):
            table = jnp.where(q // 2 == i, total[0:1, 128 * i:128 * (i + 1)], table)
        table = jnp.where(q % 2 == 1, pltpu.roll(table, 64, 1), table)
        return table, total

    def tile_sum(buf, n):
        total = buf[0]
        for i in range(1, n):
            total = total + buf[i]
        return total

    def apply(slot, planes):
        images = []
        for j in range(cz):
            below = planes[j - 1] if j > 0 else zhalo[slot, 0]
            above = planes[j + 1] if j < cz - 1 else zhalo[slot, 1]
            v = planes[j]
            images.append(
                diag[j] * v - kz[j] * below - kz[j + 1] * above
                - kyl[j] * y_below(slot, v, j) - kyh[j] * y_above(slot, v, j)
                - kxl[j] * pltpu.roll(v, 1, 1) - kxh[j] * pltpu.roll(v, nx - 1, 1))
        return images

    couple = cpl_ref[0]
    cg[k] = jnp.where(k % 2 == 1, couple, couple.T)
    for j in range(cz):
        zz[j] = 1.0 / (gain_ref[j] * (0.001 + 0.999 * phase_ref[j].astype(F32)))
    for slot in range(3):
        halo_clear(slot)
    pl.semaphore_wait(barrier, ns - 1 + nq - 1)
    halo_start(0, zz)
    gather_start("slab", k, ns, cg, cg_ss, cg_rs)

    for j in range(cz):
        label = sub_ref[j]
        high, low = label // 8, label % 8
        for h in range(8):
            hot_hi[j, h] = jnp.where(high == h, 1.0, 0.0).astype(BF16)
        digit = lax.broadcasted_iota(jnp.int32, (8, nx), 0)
        hot_lo[j] = jnp.concatenate(
            [jnp.where(low[y:y + 1] == digit, 1.0, 0.0) for y in range(cy)], axis=0).astype(BF16)

    right_side = [b_ref[j] for j in range(cz)]
    first_in = restrict(right_side)

    m = [zz[j] for j in range(cz)]
    kx_lo = []
    for j in range(cz):
        lo = jnp.where(lane == 0, m[j], harmonic(m[j], pltpu.roll(m[j], 1, 1)))
        hi = jnp.where(lane == nx - 1, m[j], pltpu.roll(lo, nx - 1, 1))
        kx_lo.append(lo + hi)
        kxl[j] = jnp.where(lane == 0, 0.0, lo)
        kxh[j] = jnp.where(lane == nx - 1, 0.0, hi)
    halo_wait(0, zz)
    kz[0] = harmonic(m[0], zhalo[0, 0])
    for j in range(1, cz):
        kz[j] = harmonic(m[j - 1], m[j])
    kz[cz] = harmonic(m[cz - 1], zhalo[0, 1])
    for j in range(cz):
        lo = harmonic(m[j], y_below(0, m[j], j))
        last = harmonic(m[j][cy - 1:cy], yhalo[0, 1, j:j + 1])
        hi = jnp.where(row == cy - 1, last, pltpu.roll(lo, cy - 1, 0))
        kyl[j] = lo
        kyh[j] = hi
        diag[j] = kz[j] + kz[j + 1] + lo + hi + kx_lo[j]
    previous = None
    for j in range(LINE):
        denom = diag[j] if j == 0 else diag[j] + kz[j] * previous
        inverse = 1.0 / denom
        inv[j] = inverse
        if j < LINE - 1:
            previous = -kz[j + 1] * inverse
            gam[j] = previous

    block = solve_lines(right_side)
    for j in range(cz):
        bj[j] = block[j]
    qbuf[0, q] = message(first_in, partial(right_side, block))
    gather_start("quad", q, nq, qbuf.at[0], q_ss.at[0], q_rs.at[0])
    gather_wait("quad", q, nq, qbuf.at[0], q_ss.at[0], q_rs.at[0])
    sbuf[0, k] = message(coarse_rhs(0), tile_sum(qbuf.at[0], nq)[1:2])
    gather_start("slab", k, ns, sbuf.at[0], s_ss.at[0], s_rs.at[0])
    gather_wait("slab", k, ns, cg, cg_ss, cg_rs)
    gather_wait("slab", k, ns, sbuf.at[0], s_ss.at[0], s_rs.at[0])
    rhs_first = [sbuf[0, i, 0:1] for i in range(ns)]
    share, square = chain(rhs_first)
    sub_wide = lax.broadcasted_iota(jnp.int32, (8, nq * count), 0)
    rbuf[0, q] = jnp.where(sub_wide == 0, share, square)
    gather_start("quad", q, nq, rbuf.at[0], r_ss.at[0], r_rs.at[0])
    rz_block = jnp.sum(tile_sum(sbuf.at[0], ns)[1:2], axis=1, keepdims=True)
    gather_wait("quad", q, nq, rbuf.at[0], r_ss.at[0], r_rs.at[0])
    table, total = own_table(0)
    rz = rz_block + total[1:2, 0:1]
    for j in range(cz):
        p0[j] = bj[j] + interpolate(table, j)
    halo_start(1, p0)
    halo_wait(1, p0)
    direction = [p0[j] for j in range(cz)]
    image = apply(1, direction)
    for j in range(cz):
        q0[j] = image[j]

    qbuf[1, q] = message(restrict(image), partial(direction, image))
    gather_start("quad", q, nq, qbuf.at[1], q_ss.at[1], q_rs.at[1])
    image_block = solve_lines([q0[j] for j in range(cz)])
    for j in range(cz):
        zz[j] = image_block[j]
    gather_wait("quad", q, nq, qbuf.at[1], q_ss.at[1], q_rs.at[1])
    sbuf[1, k] = message(coarse_rhs(1), tile_sum(qbuf.at[1], nq)[1:2])
    gather_start("slab", k, ns, sbuf.at[1], s_ss.at[1], s_rs.at[1])
    gather_wait("slab", k, ns, sbuf.at[1], s_ss.at[1], s_rs.at[1])
    alpha = rz / jnp.sum(tile_sum(sbuf.at[1], ns)[1:2], axis=1, keepdims=True)
    share, square = chain([sbuf[0, i, 0:1] - alpha * sbuf[1, i, 0:1] for i in range(ns)])
    resid = [b_ref[j] - alpha * q0[j] for j in range(cz)]
    block = [bj[j] - alpha * zz[j] for j in range(cz)]
    for j in range(cz):
        r_ref[j] = resid[j]
        bj[j] = block[j]
    dots = jnp.concatenate([partial(resid, block)] + [jnp.zeros((1, 128), F32)] * (nq * count // 128 - 1), axis=1)
    rbuf[1, q] = jnp.where(sub_wide == 0, share, jnp.where(sub_wide == 1, square, dots))
    gather_start("quad", q, nq, rbuf.at[1], r_ss.at[1], r_rs.at[1])
    gather_wait("quad", q, nq, rbuf.at[1], r_ss.at[1], r_rs.at[1])
    table, total = own_table(1)
    dbuf[k] = jnp.broadcast_to(total[2:3, :128], (8, 128))
    gather_start("slab", k, ns, dbuf, d_ss, d_rs)
    for j in range(cz):
        zz[j] = bj[j] + interpolate(table, j)
    halo_start(2, zz)
    halo_wait(2, zz)
    image = apply(2, [zz[j] for j in range(cz)])
    gather_wait("slab", k, ns, dbuf, d_ss, d_rs)
    rz_next = total[1:2, 0:1] + jnp.sum(tile_sum(dbuf, ns)[0:1], axis=1, keepdims=True)
    beta = rz_next / rz
    direction = [zz[j] + beta * p0[j] for j in range(cz)]
    image = [image[j] + beta * q0[j] for j in range(cz)]
    ebuf[q] = jnp.broadcast_to(partial(direction, image), (8, 128))
    gather_start("quad", q, nq, ebuf, e_ss, e_rs)
    for j in range(cz):
        zz[j] = direction[j]
        q0[j] = image[j]
        x_ref[j] = alpha * p0[j]
    gather_wait("quad", q, nq, ebuf, e_ss, e_rs)
    fbuf[k] = tile_sum(ebuf, nq)
    gather_start("slab", k, ns, fbuf, f_ss, f_rs)
    gather_wait("slab", k, ns, fbuf, f_ss, f_rs)
    last = rz_next / jnp.sum(tile_sum(fbuf, ns)[0:1], axis=1, keepdims=True)
    for j in range(cz):
        x_ref[j] = x_ref[j] + last * zz[j]
        r_ref[j] = r_ref[j] - last * q0[j]
    for c in pending:
        c.wait_send()


def solution(mesh):
    ns, nq = mesh.shape["slab"], mesh.shape["quad"]

    def body(right_side, phase_label, density_gain, subdomain, block_factor, coupling):
        cz, cy, nx = right_side.shape
        count = coupling.shape[2]
        field = pltpu.VMEM((cz, cy, nx), F32)
        dma = pltpu.SemaphoreType.DMA
        shape = jax.ShapeDtypeStruct((cz, cy, nx), F32)
        return tuple(pl.pallas_call(
            functools.partial(kernel, ns, nq),
            out_shape=(shape, shape),
            in_specs=[pl.BlockSpec(memory_space=pltpu.VMEM)] * 6,
            out_specs=(pl.BlockSpec(memory_space=pltpu.VMEM),) * 2,
            scratch_shapes=[
                pltpu.VMEM((cz + 1, cy, nx), F32), field, field, field, field, field, field, field,
                pltpu.VMEM((cz, 8, cy, nx), BF16), pltpu.VMEM((cz, 8 * cy, nx), BF16),
                field, field, field, field,
                pltpu.VMEM((ns, count, count), F32),
                pltpu.VMEM((2, nq, 8, 128), F32), pltpu.VMEM((2, ns, 8, 128), F32),
                pltpu.VMEM((2, nq, 8, nq * count), F32), pltpu.VMEM((ns, 8, 128), F32),
                pltpu.VMEM((nq, 8, 128), F32), pltpu.VMEM((ns, 8, 128), F32),
                pltpu.VMEM((3, 2, cy, nx), F32), pltpu.VMEM((3, 2, cz, nx), F32), pltpu.VMEM((3, 2, cz, nx), F32),
                dma((ns,)), dma((ns,)), dma((2, nq)), dma((2, nq)), dma((2, ns)), dma((2, ns)),
                dma((2, nq)), dma((2, nq)), dma((ns,)), dma((ns,)), dma((nq,)), dma((nq,)),
                dma((ns,)), dma((ns,)), dma((3, 4)), dma((3, 4)),
            ],
            compiler_params=pltpu.CompilerParams(
                collective_id=0, has_side_effects=True, vmem_limit_bytes=40 * 1024 * 1024),
        )(right_side, phase_label, density_gain, subdomain, block_factor, coupling))

    spec = P("slab", "quad", None)
    return jax.shard_map(body, mesh=mesh, in_specs=(spec,) * 6, out_specs=(spec, spec), check_vma=False)
```

```python
import functools

import jax
import jax.numpy as jnp
from jax import lax
from jax.experimental import pallas as pl
from jax.experimental.pallas import tpu as pltpu
from jax.sharding import PartitionSpec as P

LINE = 4
ITERS = 2
MESH = pl.DeviceIdType.MESH
F32 = jnp.float32
BF16 = jnp.bfloat16


def kernel(ns, nq, b_hbm, phase_hbm, gain_hbm, sub_hbm, fac_hbm, cpl_hbm, x_out, p_out, r_out, q_out, step_ref,
           b_ref, phase_ref, gain_ref, sub_ref, fac_ref, cpl_ref, x_ref, r_ref, in_sem, out_sem, kz, kyl, kyh, kxl, kxh, diag, inv, gam, hot_hi, hot_lo, p0, q0, bj, zz,
           cg, cgw, qbuf, sbuf, rbuf, ebuf, fbuf, zhalo, yhalo, ysend,
           cg_ss, cg_rs, q_ss, q_rs, s_ss, s_rs, r_ss, r_rs, e_ss, e_rs, f_ss, f_rs, h_ss, h_rs):
    k = lax.axis_index("slab")
    q = lax.axis_index("quad")
    cz, cy, nx = b_ref.shape
    count = cpl_ref.shape[2]
    pending = []
    loads = [pltpu.make_async_copy(src, dst, in_sem.at[i]) for i, (src, dst) in enumerate((
        (phase_hbm, phase_ref), (gain_hbm, gain_ref), (cpl_hbm, cpl_ref),
        (sub_hbm, sub_ref), (b_hbm, b_ref), (fac_hbm, fac_ref)))]
    for c in loads:
        c.start()

    barrier = pltpu.get_barrier_semaphore()
    for d in range(1, ns):
        pl.semaphore_signal(barrier, inc=1, device_id={"slab": lax.rem(k + d, ns)}, device_id_type=MESH)
    for d in range(1, nq):
        pl.semaphore_signal(barrier, inc=1, device_id={"quad": lax.rem(q + d, nq)}, device_id_type=MESH)

    def copies(axis, me, n, buf, ss, rs):
        out = []
        for d in range(1, n):
            out.append(pltpu.make_async_remote_copy(
                src_ref=buf.at[me], dst_ref=buf.at[me], send_sem=ss.at[d], recv_sem=rs.at[d],
                device_id={axis: lax.rem(me + d, n)}, device_id_type=MESH))
        return out

    def gather_start(axis, me, n, buf, ss, rs):
        for c in copies(axis, me, n, buf, ss, rs):
            c.start()
            pending.append(c)

    def gather_wait(axis, me, n, buf, ss, rs):
        for d in range(1, n):
            at = lax.rem(me + n - d, n)
            pltpu.make_async_remote_copy(
                src_ref=buf.at[at], dst_ref=buf.at[at], send_sem=ss.at[d], recv_sem=rs.at[d],
                device_id={axis: at}, device_id_type=MESH).wait_recv()

    row = lax.broadcasted_iota(jnp.int32, (cy, nx), 0)
    lane = lax.broadcasted_iota(jnp.int32, (cy, nx), 1)
    sub8 = lax.broadcasted_iota(jnp.int32, (8, 128), 0)
    lane8 = lax.broadcasted_iota(jnp.int32, (8, 128), 1)
    eye = (lax.broadcasted_iota(jnp.int32, (count, count), 0)
           == lax.broadcasted_iota(jnp.int32, (count, count), 1)).astype(F32)

    def halo_parts(slot, src):
        up, down = jnp.minimum(k + 1, ns - 1), jnp.maximum(k - 1, 0)
        right, left = jnp.minimum(q + 1, nq - 1), jnp.maximum(q - 1, 0)

        def copy(s, dst, i, axis, to):
            return pltpu.make_async_remote_copy(
                src_ref=s, dst_ref=dst, send_sem=h_ss.at[slot, i], recv_sem=h_rs.at[slot, i],
                device_id={axis: to}, device_id_type=MESH)

        return (
            (k < ns - 1, k > 0, copy(src.at[cz - 1], zhalo.at[slot, 0], 0, "slab", up)),
            (k > 0, k < ns - 1, copy(src.at[0], zhalo.at[slot, 1], 1, "slab", down)),
            (q < nq - 1, q > 0, copy(ysend.at[slot, 1], yhalo.at[slot, 0], 2, "quad", right)),
            (q > 0, q < nq - 1, copy(ysend.at[slot, 0], yhalo.at[slot, 1], 3, "quad", left)),
        )

    def halo_clear(slot):
        for buf, i, edge in ((zhalo, 0, k == 0), (zhalo, 1, k == ns - 1),
                             (yhalo, 0, q == 0), (yhalo, 1, q == nq - 1)):
            @pl.when(edge)
            def _(buf=buf, i=i):
                buf[slot, i] = jnp.zeros(buf.shape[2:], F32)

    def halo_start(slot, src):
        for j in range(cz):
            ysend[slot, 0, j:j + 1] = src[j, 0:1]
            ysend[slot, 1, j:j + 1] = src[j, cy - 1:cy]
        for sends, unused, c in halo_parts(slot, src):
            @pl.when(sends)
            def _(c=c):
                c.start()

    def halo_wait(slot, src):
        for sends, receives, c in halo_parts(slot, src):
            @pl.when(receives)
            def _(c=c):
                c.wait_recv()

            @pl.when(sends)
            def _(c=c):
                c.wait_send()

    def y_below(slot, plane, j):
        return jnp.where(row == 0, yhalo[slot, 0, j:j + 1], pltpu.roll(plane, 1, 0))

    def y_above(slot, plane, j):
        return jnp.where(row == cy - 1, yhalo[slot, 1, j:j + 1], pltpu.roll(plane, cy - 1, 0))

    def harmonic(here, there):
        return jnp.where(there > 0, 2.0 * here * there / (here + there), here)

    def restrict(planes):
        total = None
        for j in range(cz):
            high = planes[j].astype(BF16)
            low = (planes[j] - high.astype(F32)).astype(BF16)
            lhs = jnp.concatenate([part * hot_hi[j, h] for part in (high, low) for h in range(8)], axis=0)
            now = lax.dot_general(lhs, hot_lo[j], (((1,), (1,)), ((), ())), preferred_element_type=F32)
            total = now if total is None else total + now
        total = total[:8 * cy] + total[8 * cy:]
        spot = lax.broadcasted_iota(jnp.int32, total.shape, 0) % cy
        across = lax.broadcasted_iota(jnp.int32, total.shape, 1) // 8
        total = jnp.where(spot == across, total, 0.0)
        tile = jnp.concatenate(
            [jnp.sum(total[cy * h:cy * (h + 1)], axis=0, keepdims=True) for h in range(8)], axis=0)
        for shift in (8, 16, 32, 64):
            tile = tile + pltpu.roll(tile, shift, 1)
        return jnp.sum(jnp.where(sub8 == lane8 // 8, tile, 0.0), axis=0, keepdims=True)

    def partial(left, right):
        total = left[0] * right[0]
        for j in range(1, cz):
            total = total + left[j] * right[j]
        total = total[:8] + total[8:]
        tile = total[:, :128]
        for c in range(1, nx // 128):
            tile = tile + total[:, 128 * c:128 * (c + 1)]
        return jnp.sum(tile, axis=0, keepdims=True)

    def solve_lines(planes):
        rho = [planes[0] * inv[0]]
        for j in range(1, LINE):
            rho.append((planes[j] + kz[j] * rho[j - 1]) * inv[j])
        values = [None] * LINE
        values[LINE - 1] = rho[LINE - 1]
        for j in range(LINE - 2, -1, -1):
            values[j] = rho[j] - gam[j] * values[j + 1]
        return values

    def message(first, second):
        return jnp.where(sub8 == 0, first, second)

    def coarse_rhs(slot):
        rows = [qbuf[slot, i, 0:1] for i in range(nq)]
        pieces = [rows[2 * i] + pltpu.roll(rows[2 * i + 1], 64, 1) for i in range(nq // 2)]
        whole = jnp.concatenate(pieces, axis=1)
        column = jnp.sum(fac_ref[0] * whole, axis=1, keepdims=True)
        return jnp.sum(jnp.concatenate([eye, jnp.zeros_like(eye)], axis=1) * column, axis=0, keepdims=True)

    def chain(rhs):
        us = [rhs[0][:, :count]]
        sq_row, sq_col = us[0] * us[0], None
        for i in range(1, ns):
            if i % 2:
                now = jnp.sum(cg[i] * us[i - 1] + eye * rhs[i][:, :count], axis=1, keepdims=True)
                sq_col = now * now if sq_col is None else sq_col + now * now
            else:
                now = jnp.sum(cg[i] * us[i - 1], axis=0, keepdims=True) + rhs[i][:, :count]
                sq_row = sq_row + now * now
            us.append(now)
        w = us[ns - 1]
        own_row = jnp.zeros((1, count), F32)
        own_col = jnp.where(k == ns - 1, w, 0.0)
        for i in range(ns - 1, 0, -1):
            if i % 2:
                w = jnp.sum(cg[i] * w, axis=0, keepdims=True) + us[i - 1]
                own_row = jnp.where(k == i - 1, w, own_row)
            else:
                w = jnp.sum(cg[i] * w, axis=1, keepdims=True) + us[i - 1]
                own_col = jnp.where(k == i - 1, w, own_col)
        own = own_col + jnp.sum(eye * own_row, axis=1, keepdims=True)
        square = jnp.sum(sq_row, axis=1, keepdims=True) + jnp.sum(sq_col, axis=0, keepdims=True)
        share = jnp.sum(fac_ref[0] * own, axis=0, keepdims=True)
        return share, square

    def interpolate(table, j):
        wide = jnp.broadcast_to(table, (cy, 128))
        return jnp.concatenate(
            [jnp.take_along_axis(wide, sub_ref[j, :, 128 * c:128 * (c + 1)], axis=1, mode="promise_in_bounds")
             for c in range(nx // 128)], axis=1)

    def own_table(slot):
        total = rbuf[slot, 0]
        for i in range(1, nq):
            total = total + rbuf[slot, i]
        table = total[0:1, :128]
        for i in range(1, nq // 2):
            table = jnp.where(q // 2 == i, total[0:1, 128 * i:128 * (i + 1)], table)
        table = jnp.where(q % 2 == 1, pltpu.roll(table, 64, 1), table)
        return table, total

    def tile_sum(buf, n):
        total = buf[0]
        for i in range(1, n):
            total = total + buf[i]
        return total

    def apply(slot, planes):
        images = []
        for j in range(cz):
            below = planes[j - 1] if j > 0 else zhalo[slot, 0]
            above = planes[j + 1] if j < cz - 1 else zhalo[slot, 1]
            v = planes[j]
            images.append(
                diag[j] * v - kz[j] * below - kz[j + 1] * above
                - kyl[j] * y_below(slot, v, j) - kyh[j] * y_above(slot, v, j)
                - kxl[j] * pltpu.roll(v, 1, 1) - kxh[j] * pltpu.roll(v, nx - 1, 1))
        return images

    for slot in range(3):
        halo_clear(slot)
    loads[0].wait()
    loads[1].wait()
    for j in range(cz):
        zz[j] = 1.0 / (gain_ref[j] * (0.001 + 0.999 * phase_ref[j].astype(F32)))
    pl.semaphore_wait(barrier, ns - 1 + nq - 1)
    halo_start(0, zz)
    loads[2].wait()
    couple = cpl_ref[0]
    couple = jnp.where(k % 2 == 1, couple, couple.T)
    cgw[k] = jnp.concatenate([couple[:count // 2], couple[count // 2:]], axis=1)
    gather_start("slab", k, ns, cgw, cg_ss, cg_rs)

    loads[3].wait()
    loads[4].wait()
    for j in range(cz):
        label = sub_ref[j]
        high, low = label >> 3, label & 7
        for h in range(8):
            hot_hi[j, h] = jnp.where(high == h, 1.0, 0.0).astype(BF16)
        digit = lax.broadcasted_iota(jnp.int32, (8, nx), 0)
        hot_lo[j] = jnp.concatenate(
            [jnp.where(low[y:y + 1] == digit, 1.0, 0.0) for y in range(cy)], axis=0).astype(BF16)

    right_side = [b_ref[j] for j in range(cz)]
    qbuf[0, q] = jnp.broadcast_to(restrict(right_side), (8, 128))
    gather_start("quad", q, nq, qbuf.at[0], q_ss.at[0], q_rs.at[0])

    m = [zz[j] for j in range(cz)]
    kx_lo = []
    for j in range(cz):
        lo = jnp.where(lane == 0, m[j], harmonic(m[j], pltpu.roll(m[j], 1, 1)))
        hi = jnp.where(lane == nx - 1, m[j], pltpu.roll(lo, nx - 1, 1))
        kx_lo.append(lo + hi)
        kxl[j] = jnp.where(lane == 0, 0.0, lo)
        kxh[j] = jnp.where(lane == nx - 1, 0.0, hi)
    halo_wait(0, zz)
    kz[0] = harmonic(m[0], zhalo[0, 0])
    for j in range(1, cz):
        kz[j] = harmonic(m[j - 1], m[j])
    kz[cz] = harmonic(m[cz - 1], zhalo[0, 1])
    for j in range(cz):
        lo = harmonic(m[j], y_below(0, m[j], j))
        last = harmonic(m[j][cy - 1:cy], yhalo[0, 1, j:j + 1])
        hi = jnp.where(row == cy - 1, last, pltpu.roll(lo, cy - 1, 0))
        kyl[j] = lo
        kyh[j] = hi
        diag[j] = kz[j] + kz[j + 1] + lo + hi + kx_lo[j]
    previous = None
    for j in range(LINE):
        denom = diag[j] if j == 0 else diag[j] + kz[j] * previous
        inverse = 1.0 / denom
        inv[j] = inverse
        if j < LINE - 1:
            previous = -kz[j + 1] * inverse
            gam[j] = previous

    block = solve_lines(right_side)
    for j in range(cz):
        bj[j] = block[j]
    own_dot = partial(right_side, block)
    loads[5].wait()
    gather_wait("quad", q, nq, qbuf.at[0], q_ss.at[0], q_rs.at[0])
    sbuf[0, k] = message(coarse_rhs(0), own_dot)
    gather_start("slab", k, ns, sbuf.at[0], s_ss.at[0], s_rs.at[0])
    gather_wait("slab", k, ns, cgw, cg_ss, cg_rs)
    for i in range(ns):
        cg[i, :count // 2] = cgw[i, :, :count]
        cg[i, count // 2:] = cgw[i, :, count:]
    gather_wait("slab", k, ns, sbuf.at[0], s_ss.at[0], s_rs.at[0])
    rhs_first = [sbuf[0, i, 0:1] for i in range(ns)]
    share, square = chain(rhs_first)
    slab_dot = jnp.sum(tile_sum(sbuf.at[0], ns)[1:2], axis=1, keepdims=True)
    sub_wide = lax.broadcasted_iota(jnp.int32, (8, nq * count), 0)
    rbuf[0, q] = jnp.where(sub_wide == 0, share, square + slab_dot)
    gather_start("quad", q, nq, rbuf.at[0], r_ss.at[0], r_rs.at[0])
    gather_wait("quad", q, nq, rbuf.at[0], r_ss.at[0], r_rs.at[0])
    table, total = own_table(0)
    rz = total[1:2, 0:1]
    for j in range(cz):
        p0[j] = bj[j] + interpolate(table, j)
    halo_start(1, p0)
    halo_wait(1, p0)
    direction = [p0[j] for j in range(cz)]
    image = apply(1, direction)
    for j in range(cz):
        q0[j] = image[j]

    qbuf[1, q] = message(restrict(image), partial(direction, image))
    gather_start("quad", q, nq, qbuf.at[1], q_ss.at[1], q_rs.at[1])
    image = [q0[j] for j in range(cz)]
    image_block = solve_lines(image)
    for j in range(cz):
        zz[j] = image_block[j]
    cross, own_dot = partial(image, [bj[j] for j in range(cz)]), partial(image, image_block)
    gather_wait("quad", q, nq, qbuf.at[1], q_ss.at[1], q_rs.at[1])
    sbuf[1, k] = jnp.where(sub8 < 2, message(coarse_rhs(1), tile_sum(qbuf.at[1], nq)[1:2]),
                           jnp.where(sub8 == 2, cross, own_dot))
    gather_start("slab", k, ns, sbuf.at[1], s_ss.at[1], s_rs.at[1])
    gather_wait("slab", k, ns, sbuf.at[1], s_ss.at[1], s_rs.at[1])
    sums = jnp.sum(tile_sum(sbuf.at[1], ns), axis=1, keepdims=True)
    alpha = rz / sums[1:2]
    share, square = chain([sbuf[0, i, 0:1] - alpha * sbuf[1, i, 0:1] for i in range(ns)])
    square = square + slab_dot - 2.0 * alpha * sums[2:3] + alpha * alpha * sums[3:4]
    rbuf[1, q] = jnp.where(sub_wide == 0, share, square)
    gather_start("quad", q, nq, rbuf.at[1], r_ss.at[1], r_rs.at[1])
    for j in range(cz):
        r_ref[j] = b_ref[j] - alpha * q0[j]
        x_ref[j] = alpha * p0[j]
        bj[j] = bj[j] - alpha * zz[j]
    outs = [pltpu.make_async_copy(src, dst, out_sem.at[i]) for i, (src, dst) in enumerate((
        (x_ref, x_out), (zz, p_out), (r_ref, r_out), (q0, q_out)))]
    outs[0].start()
    outs[2].start()
    gather_wait("quad", q, nq, rbuf.at[1], r_ss.at[1], r_rs.at[1])
    table, total = own_table(1)
    rz_next = total[1:2, 0:1]
    beta = rz_next / rz
    for j in range(cz):
        zz[j] = bj[j] + interpolate(table, j) + beta * p0[j]
    halo_start(2, zz)
    halo_wait(2, zz)
    direction = [zz[j] for j in range(cz)]
    image = apply(2, direction)
    ebuf[q] = jnp.broadcast_to(partial(direction, image), (8, 128))
    gather_start("quad", q, nq, ebuf, e_ss, e_rs)
    for j in range(cz):
        q0[j] = image[j]
    outs[1].start()
    outs[3].start()
    gather_wait("quad", q, nq, ebuf, e_ss, e_rs)
    fbuf[k] = tile_sum(ebuf, nq)
    gather_start("slab", k, ns, fbuf, f_ss, f_rs)
    gather_wait("slab", k, ns, fbuf, f_ss, f_rs)
    last = rz_next / jnp.sum(tile_sum(fbuf, ns)[0:1], axis=1, keepdims=True)
    step_ref[...] = jnp.broadcast_to(last, (1, nx))
    for c in outs:
        c.wait()
    for c in pending:
        c.wait_send()


def solution(mesh):
    ns, nq = mesh.shape["slab"], mesh.shape["quad"]

    def body(right_side, phase_label, density_gain, subdomain, block_factor, coupling):
        cz, cy, nx = right_side.shape
        count = coupling.shape[2]
        field = pltpu.VMEM((cz, cy, nx), F32)
        dma = pltpu.SemaphoreType.DMA
        shape = jax.ShapeDtypeStruct((cz, cy, nx), F32)
        hbm = pl.BlockSpec(memory_space=pltpu.HBM)
        x_part, p_part, r_part, q_part, step = pl.pallas_call(
            functools.partial(kernel, ns, nq),
            out_shape=(shape, shape, shape, shape, jax.ShapeDtypeStruct((1, nx), F32)),
            in_specs=[hbm] * 6,
            out_specs=(hbm,) * 4 + (pl.BlockSpec(memory_space=pltpu.VMEM),),
            scratch_shapes=[
                field, pltpu.VMEM((cz, cy, nx), jnp.int32), field, pltpu.VMEM((cz, cy, nx), jnp.int32),
                pltpu.VMEM(block_factor.shape, F32), pltpu.VMEM(coupling.shape, F32), field, field,
                dma((6,)), dma((4,)),
                pltpu.VMEM((cz + 1, cy, nx), F32), field, field, field, field, field, field, field,
                pltpu.VMEM((cz, 8, cy, nx), BF16), pltpu.VMEM((cz, 8 * cy, nx), BF16),
                field, field, field, field,
                pltpu.VMEM((ns, count, count), F32), pltpu.VMEM((ns, count // 2, 2 * count), F32),
                pltpu.VMEM((2, nq, 8, 128), F32), pltpu.VMEM((2, ns, 8, 128), F32),
                pltpu.VMEM((2, nq, 8, nq * count), F32),
                pltpu.VMEM((nq, 8, 128), F32), pltpu.VMEM((ns, 8, 128), F32),
                pltpu.VMEM((3, 2, cy, nx), F32), pltpu.VMEM((3, 2, cz, nx), F32), pltpu.VMEM((3, 2, cz, nx), F32),
                dma((ns,)), dma((ns,)), dma((2, nq)), dma((2, nq)), dma((2, ns)), dma((2, ns)),
                dma((2, nq)), dma((2, nq)), dma((nq,)), dma((nq,)),
                dma((ns,)), dma((ns,)), dma((3, 4)), dma((3, 4)),
            ],
            compiler_params=pltpu.CompilerParams(
                collective_id=0, has_side_effects=True, vmem_limit_bytes=40 * 1024 * 1024),
        )(*(pltpu.with_memory_space_constraint(value, pltpu.HBM) for value in (
            right_side, phase_label, density_gain, subdomain, block_factor, coupling)))
        return x_part + step * p_part, r_part - step * q_part

    spec = P("slab", "quad", None)
    return jax.shard_map(body, mesh=mesh, in_specs=(spec,) * 6, out_specs=(spec, spec), check_vma=False)
```

```python
import functools

import jax
import jax.numpy as jnp
from jax import lax
from jax.experimental import pallas as pl
from jax.experimental.pallas import tpu as pltpu
from jax.sharding import PartitionSpec as P

LINE = 4
ITERS = 2
MESH = pl.DeviceIdType.MESH
F32 = jnp.float32
BF16 = jnp.bfloat16


def kernel(ns, nq, b_hbm, phase_hbm, gain_hbm, sub_hbm, fac_hbm, cpl_hbm, x_out, p_out, r_out, q_out, step_ref,
           b_ref, phase_ref, gain_ref, sub_ref, fac_ref, cpl_ref, x_ref, r_ref, in_sem, out_sem, kz, kyl, kyh, kxl, kxh, diag, inv, gam, hot_hi, hot_lo, p0, q0, bj, zz,
           cg, cgw, qbuf, sbuf, rbuf, ebuf, fbuf, zhalo, yhalo, ysend,
           fach, zsub, ysub, ysend_sub, zp, zq, yp,
           cg_ss, cg_rs, q_ss, q_rs, s_ss, s_rs, r_ss, r_rs, e_ss, e_rs, f_ss, f_rs, h_ss, h_rs):
    k = lax.axis_index("slab")
    q = lax.axis_index("quad")
    cz, cy, nx = b_ref.shape
    count = cpl_ref.shape[2]
    pending = []
    loads = [pltpu.make_async_copy(src, dst, in_sem.at[i]) for i, (src, dst) in enumerate((
        (phase_hbm, phase_ref), (gain_hbm, gain_ref), (cpl_hbm, cpl_ref),
        (sub_hbm, sub_ref), (b_hbm, b_ref), (fac_hbm, fac_ref)))]
    for c in loads:
        c.start()

    barrier = pltpu.get_barrier_semaphore()
    for d in range(1, ns):
        pl.semaphore_signal(barrier, inc=1, device_id={"slab": lax.rem(k + d, ns)}, device_id_type=MESH)
    for d in range(1, nq):
        pl.semaphore_signal(barrier, inc=1, device_id={"quad": lax.rem(q + d, nq)}, device_id_type=MESH)

    def copies(axis, me, n, buf, ss, rs):
        out = []
        for d in range(1, n):
            out.append(pltpu.make_async_remote_copy(
                src_ref=buf.at[me], dst_ref=buf.at[me], send_sem=ss.at[d], recv_sem=rs.at[d],
                device_id={axis: lax.rem(me + d, n)}, device_id_type=MESH))
        return out

    def gather_start(axis, me, n, buf, ss, rs):
        for c in copies(axis, me, n, buf, ss, rs):
            c.start()
            pending.append(c)

    def gather_wait(axis, me, n, buf, ss, rs):
        for d in range(1, n):
            at = lax.rem(me + n - d, n)
            pltpu.make_async_remote_copy(
                src_ref=buf.at[at], dst_ref=buf.at[at], send_sem=ss.at[d], recv_sem=rs.at[d],
                device_id={axis: at}, device_id_type=MESH).wait_recv()

    row = lax.broadcasted_iota(jnp.int32, (cy, nx), 0)
    lane = lax.broadcasted_iota(jnp.int32, (cy, nx), 1)
    sub8 = lax.broadcasted_iota(jnp.int32, (8, 128), 0)
    lane8 = lax.broadcasted_iota(jnp.int32, (8, 128), 1)
    eye = (lax.broadcasted_iota(jnp.int32, (count, count), 0)
           == lax.broadcasted_iota(jnp.int32, (count, count), 1)).astype(F32)

    halos = [(zhalo.at[i], yhalo.at[i], ysend.at[i]) for i in range(3)] + [(zsub, ysub, ysend_sub)]

    def halo_parts(slot, src):
        up, down = jnp.minimum(k + 1, ns - 1), jnp.maximum(k - 1, 0)
        right, left = jnp.minimum(q + 1, nq - 1), jnp.maximum(q - 1, 0)

        def copy(s, dst, i, axis, to):
            return pltpu.make_async_remote_copy(
                src_ref=s, dst_ref=dst, send_sem=h_ss.at[slot, i], recv_sem=h_rs.at[slot, i],
                device_id={axis: to}, device_id_type=MESH)

        if slot == 4:
            return ((k < ns - 1, k > 0, copy(src, fach.at[0], 0, "slab", up)),
                    (k > 0, k < ns - 1, copy(src, fach.at[1], 1, "slab", down)))
        zdst, ydst, ysrc = halos[slot]
        return (
            (k < ns - 1, k > 0, copy(src.at[cz - 1], zdst.at[0], 0, "slab", up)),
            (k > 0, k < ns - 1, copy(src.at[0], zdst.at[1], 1, "slab", down)),
            (q < nq - 1, q > 0, copy(ysrc.at[1], ydst.at[0], 2, "quad", right)),
            (q > 0, q < nq - 1, copy(ysrc.at[0], ydst.at[1], 3, "quad", left)),
        )

    def halo_clear():
        for zdst, ydst, unused in halos:
            for buf, i, edge in ((zdst, 0, k == 0), (zdst, 1, k == ns - 1),
                                 (ydst, 0, q == 0), (ydst, 1, q == nq - 1)):
                @pl.when(edge)
                def _(buf=buf, i=i):
                    buf[i] = jnp.zeros(buf.shape[1:], buf.dtype)
        for i, edge in ((0, k == 0), (1, k == ns - 1)):
            @pl.when(edge)
            def _(i=i):
                fach[i] = jnp.zeros(fach.shape[1:], F32)

    def halo_start(slot, src):
        if slot < 4:
            ysrc = halos[slot][2]
            for j in range(cz):
                ysrc[0, j:j + 1] = src[j, 0:1]
                ysrc[1, j:j + 1] = src[j, cy - 1:cy]
        for sends, unused, c in halo_parts(slot, src):
            @pl.when(sends)
            def _(c=c):
                c.start()

    def halo_wait(slot, src):
        for sends, receives, c in halo_parts(slot, src):
            @pl.when(receives)
            def _(c=c):
                c.wait_recv()

            @pl.when(sends)
            def _(c=c):
                c.wait_send()

    def y_below(plane, edge):
        return jnp.where(row == 0, edge, pltpu.roll(plane, 1, 0))

    def y_above(plane, edge):
        return jnp.where(row == cy - 1, edge, pltpu.roll(plane, cy - 1, 0))

    def harmonic(here, there):
        return jnp.where(there > 0, 2.0 * here * there / (here + there), here)

    def restrict(planes):
        total = None
        for j in range(cz):
            high = planes[j].astype(BF16)
            low = (planes[j] - high.astype(F32)).astype(BF16)
            lhs = jnp.concatenate([part * hot_hi[j, h] for part in (high, low) for h in range(8)], axis=0)
            now = lax.dot_general(lhs, hot_lo[j], (((1,), (1,)), ((), ())), preferred_element_type=F32)
            total = now if total is None else total + now
        total = total[:8 * cy] + total[8 * cy:]
        spot = lax.broadcasted_iota(jnp.int32, total.shape, 0) % cy
        across = lax.broadcasted_iota(jnp.int32, total.shape, 1) // 8
        total = jnp.where(spot == across, total, 0.0)
        tile = jnp.concatenate(
            [jnp.sum(total[cy * h:cy * (h + 1)], axis=0, keepdims=True) for h in range(8)], axis=0)
        for shift in (8, 16, 32, 64):
            tile = tile + pltpu.roll(tile, shift, 1)
        return jnp.sum(jnp.where(sub8 == lane8 // 8, tile, 0.0), axis=0, keepdims=True)

    def partial(left, right):
        total = left[0] * right[0]
        for j in range(1, cz):
            total = total + left[j] * right[j]
        total = total[:8] + total[8:]
        tile = total[:, :128]
        for c in range(1, nx // 128):
            tile = tile + total[:, 128 * c:128 * (c + 1)]
        return jnp.sum(tile, axis=0, keepdims=True)

    def solve_lines(planes):
        rho = [planes[0] * inv[0]]
        for j in range(1, LINE):
            rho.append((planes[j] + kz[j] * rho[j - 1]) * inv[j])
        values = [None] * LINE
        values[LINE - 1] = rho[LINE - 1]
        for j in range(LINE - 2, -1, -1):
            values[j] = rho[j] - gam[j] * values[j + 1]
        return values

    def message(first, second):
        return jnp.where(sub8 == 0, first, second)

    def coarse_rhs(slot):
        rows = [qbuf[slot, i, 0:1] for i in range(nq)]
        pieces = [rows[2 * i] + pltpu.roll(rows[2 * i + 1], 64, 1) for i in range(nq // 2)]
        whole = jnp.concatenate(pieces, axis=1)
        column = jnp.sum(fac_ref[0] * whole, axis=1, keepdims=True)
        return jnp.sum(jnp.concatenate([eye, jnp.zeros_like(eye)], axis=1) * column, axis=0, keepdims=True)

    def chain(rhs):
        us = [rhs[0][:, :count]]
        sq_row, sq_col = us[0] * us[0], None
        for i in range(1, ns):
            if i % 2:
                now = jnp.sum(cg[i] * us[i - 1] + eye * rhs[i][:, :count], axis=1, keepdims=True)
                sq_col = now * now if sq_col is None else sq_col + now * now
            else:
                now = jnp.sum(cg[i] * us[i - 1], axis=0, keepdims=True) + rhs[i][:, :count]
                sq_row = sq_row + now * now
            us.append(now)
        w = us[ns - 1]
        near_row = [jnp.zeros((1, count), F32)] * 3
        near_col = [jnp.where(k + d == ns - 1, w, 0.0) for d in (-1, 0, 1)]
        for i in range(ns - 1, 0, -1):
            if i % 2:
                w = jnp.sum(cg[i] * w, axis=0, keepdims=True) + us[i - 1]
                near_row = [jnp.where(k + d == i - 1, w, old) for d, old in zip((-1, 0, 1), near_row)]
            else:
                w = jnp.sum(cg[i] * w, axis=1, keepdims=True) + us[i - 1]
                near_col = [jnp.where(k + d == i - 1, w, old) for d, old in zip((-1, 0, 1), near_col)]
        near = [col + jnp.sum(eye * line, axis=1, keepdims=True) for col, line in zip(near_col, near_row)]
        square = jnp.sum(sq_row, axis=1, keepdims=True) + jnp.sum(sq_col, axis=0, keepdims=True)
        factors = (fach[0], fac_ref[0], fach[1])
        shares = [jnp.sum(f * w, axis=0, keepdims=True) for f, w in zip(factors, near)]
        return shares, square

    def pack_shares(shares, scalar):
        at = lax.broadcasted_iota(jnp.int32, (8, nq * count), 0)
        return jnp.where(at == 0, shares[0], jnp.where(at == 1, shares[1], jnp.where(at == 2, shares[2], scalar)))

    def gather_lanes(wide, index):
        return jnp.concatenate(
            [jnp.take_along_axis(wide, index[:, 128 * c:128 * (c + 1)], axis=1, mode="promise_in_bounds")
             for c in range(nx // 128)], axis=1)

    def interpolate(table, index):
        return gather_lanes(jnp.broadcast_to(table, (cy, 128)), index)

    def coarse_tables(slot):
        total = tile_sum(rbuf.at[slot], nq)

        def pick(at, quarter):
            table = jnp.zeros((1, 128), F32)
            for i in range(nq):
                piece = total[at:at + 1, 128 * (i // 2):128 * (i // 2 + 1)]
                table = jnp.where(quarter == i, pltpu.roll(piece, 64, 1) if i % 2 else piece, table)
            return table

        sides = jnp.concatenate(
            [jnp.broadcast_to(pick(1, q - 1), (cz, 128)), jnp.broadcast_to(pick(1, q + 1), (cz, 128))], axis=0)
        return pick(1, q), pick(0, q), pick(2, q), sides, total[3:4, 0:1]

    def tile_sum(buf, n):
        total = buf[0]
        for i in range(1, n):
            total = total + buf[i]
        return total

    def apply(planes):
        images = []
        for j in range(cz):
            below = planes[j - 1] if j > 0 else zp[0]
            above = planes[j + 1] if j < cz - 1 else zp[1]
            v = planes[j]
            images.append(
                diag[j] * v - kz[j] * below - kz[j + 1] * above
                - kyl[j] * y_below(v, yp[j:j + 1]) - kyh[j] * y_above(v, yp[cz + j:cz + j + 1])
                - kxl[j] * pltpu.roll(v, 1, 1) - kxh[j] * pltpu.roll(v, nx - 1, 1))
        return images

    halo_clear()
    loads[3].wait()
    loads[4].wait()
    for j in range(cz):
        label = sub_ref[j]
        high, low = label >> 3, label & 7
        for h in range(8):
            hot_hi[j, h] = jnp.where(high == h, 1.0, 0.0).astype(BF16)
        digit = lax.broadcasted_iota(jnp.int32, (8, nx), 0)
        hot_lo[j] = jnp.concatenate(
            [jnp.where(low[y:y + 1] == digit, 1.0, 0.0) for y in range(cy)], axis=0).astype(BF16)
    right_side = [b_ref[j] for j in range(cz)]
    qbuf[0, q] = jnp.broadcast_to(restrict(right_side), (8, 128))
    pl.semaphore_wait(barrier, ns - 1 + nq - 1)
    gather_start("quad", q, nq, qbuf.at[0], q_ss.at[0], q_rs.at[0])
    loads[0].wait()
    loads[1].wait()
    for j in range(cz):
        zz[j] = 1.0 / (gain_ref[j] * (0.001 + 0.999 * phase_ref[j].astype(F32)))
    halo_start(0, zz)
    loads[2].wait()
    couple = cpl_ref[0]
    couple = jnp.where(k % 2 == 1, couple, couple.T)
    cgw[k] = jnp.concatenate([couple[:count // 2], couple[count // 2:]], axis=1)
    gather_start("slab", k, ns, cgw, cg_ss, cg_rs)
    loads[5].wait()
    halo_start(4, fac_ref.at[0])

    m = [zz[j] for j in range(cz)]
    kx_lo = []
    for j in range(cz):
        lo = jnp.where(lane == 0, m[j], harmonic(m[j], pltpu.roll(m[j], 1, 1)))
        hi = jnp.where(lane == nx - 1, m[j], pltpu.roll(lo, nx - 1, 1))
        kx_lo.append(lo + hi)
        kxl[j] = jnp.where(lane == 0, 0.0, lo)
        kxh[j] = jnp.where(lane == nx - 1, 0.0, hi)
    gather_wait("quad", q, nq, qbuf.at[0], q_ss.at[0], q_rs.at[0])
    sbuf[0, k] = jnp.broadcast_to(coarse_rhs(0), (8, 128))
    gather_start("slab", k, ns, sbuf.at[0], s_ss.at[0], s_rs.at[0])
    halo_start(3, sub_ref)
    halo_wait(0, zz)
    kz[0] = harmonic(m[0], zhalo[0, 0])
    for j in range(1, cz):
        kz[j] = harmonic(m[j - 1], m[j])
    kz[cz] = harmonic(m[cz - 1], zhalo[0, 1])
    for j in range(cz):
        lo = harmonic(m[j], y_below(m[j], yhalo[0, 0, j:j + 1]))
        last = harmonic(m[j][cy - 1:cy], yhalo[0, 1, j:j + 1])
        hi = jnp.where(row == cy - 1, last, pltpu.roll(lo, cy - 1, 0))
        kyl[j] = lo
        kyh[j] = hi
        diag[j] = kz[j] + kz[j + 1] + lo + hi + kx_lo[j]
    previous = None
    for j in range(LINE):
        denom = diag[j] if j == 0 else diag[j] + kz[j] * previous
        inverse = 1.0 / denom
        inv[j] = inverse
        if j < LINE - 1:
            previous = -kz[j + 1] * inverse
            gam[j] = previous

    block = solve_lines(right_side)
    for j in range(cz):
        bj[j] = block[j]
    halo_start(1, bj)
    first_dot = partial(right_side, block)
    gather_wait("slab", k, ns, cgw, cg_ss, cg_rs)
    for i in range(ns):
        cg[i, :count // 2] = cgw[i, :, :count]
        cg[i, count // 2:] = cgw[i, :, count:]
    halo_wait(4, fac_ref.at[0])
    gather_wait("slab", k, ns, sbuf.at[0], s_ss.at[0], s_rs.at[0])
    rhs_first = [sbuf[0, i, 0:1] for i in range(ns)]
    shares, square = chain(rhs_first)
    rbuf[0, q] = pack_shares(shares, square)
    gather_start("quad", q, nq, rbuf.at[0], r_ss.at[0], r_rs.at[0])
    halo_wait(1, bj)
    halo_wait(3, sub_ref)
    ysub_all = jnp.concatenate([ysub[0], ysub[1]], axis=0)
    gather_wait("quad", q, nq, rbuf.at[0], r_ss.at[0], r_rs.at[0])
    table, before, after, sides, first_square = coarse_tables(0)
    for j in range(cz):
        p0[j] = bj[j] + interpolate(table, sub_ref[j])
    zp[0] = zhalo[1, 0] + interpolate(before, zsub[0])
    zp[1] = zhalo[1, 1] + interpolate(after, zsub[1])
    zq[0] = zp[0]
    zq[1] = zp[1]
    yp[...] = jnp.concatenate([yhalo[1, 0], yhalo[1, 1]], axis=0) + gather_lanes(sides, ysub_all)
    direction = [p0[j] for j in range(cz)]
    image = apply(direction)
    for j in range(cz):
        q0[j] = image[j]

    qbuf[1, q] = jnp.where(sub8 < 2, message(restrict(image), partial(direction, image)), first_dot)
    gather_start("quad", q, nq, qbuf.at[1], q_ss.at[1], q_rs.at[1])
    image = [q0[j] for j in range(cz)]
    image_block = solve_lines(image)
    for j in range(cz):
        zz[j] = image_block[j]
    halo_start(2, zz)
    cross, own_dot = partial(image, [bj[j] for j in range(cz)]), partial(image, image_block)
    gather_wait("quad", q, nq, qbuf.at[1], q_ss.at[1], q_rs.at[1])
    quad_sum = tile_sum(qbuf.at[1], nq)
    sbuf[1, k] = jnp.where(sub8 == 0, coarse_rhs(1), jnp.where(
        sub8 == 1, quad_sum[1:2], jnp.where(sub8 == 2, quad_sum[2:3], jnp.where(sub8 == 3, cross, own_dot))))
    gather_start("slab", k, ns, sbuf.at[1], s_ss.at[1], s_rs.at[1])
    gather_wait("slab", k, ns, sbuf.at[1], s_ss.at[1], s_rs.at[1])
    sums = jnp.sum(tile_sum(sbuf.at[1], ns), axis=1, keepdims=True)
    first_dot = sums[2:3]
    rz = first_dot + first_square
    alpha = rz / sums[1:2]
    shares, square = chain([sbuf[0, i, 0:1] - alpha * sbuf[1, i, 0:1] for i in range(ns)])
    rbuf[1, q] = pack_shares(shares, square - 2.0 * alpha * sums[3:4] + alpha * alpha * sums[4:5])
    gather_start("quad", q, nq, rbuf.at[1], r_ss.at[1], r_rs.at[1])
    for j in range(cz):
        r_ref[j] = b_ref[j] - alpha * q0[j]
        x_ref[j] = alpha * p0[j]
        bj[j] = bj[j] - alpha * zz[j]
    outs = [pltpu.make_async_copy(src, dst, out_sem.at[i]) for i, (src, dst) in enumerate((
        (x_ref, x_out), (zz, p_out), (r_ref, r_out), (q0, q_out)))]
    outs[0].start()
    outs[2].start()
    halo_wait(2, zz)
    for i in range(2):
        zp[i] = zhalo[1, i] - alpha * zhalo[2, i]
    yedge = [yhalo[1, i] - alpha * yhalo[2, i] for i in range(2)]
    gather_wait("quad", q, nq, rbuf.at[1], r_ss.at[1], r_rs.at[1])
    table, before, after, sides, last_square = coarse_tables(1)
    rz_next = first_dot + last_square
    beta = rz_next / rz
    for j in range(cz):
        zz[j] = bj[j] + interpolate(table, sub_ref[j]) + beta * p0[j]
    zp[0] = zp[0] + interpolate(before, zsub[0]) + beta * zq[0]
    zp[1] = zp[1] + interpolate(after, zsub[1]) + beta * zq[1]
    yp[...] = jnp.concatenate(yedge, axis=0) + gather_lanes(sides, ysub_all) + beta * yp[...]
    direction = [zz[j] for j in range(cz)]
    image = apply(direction)
    ebuf[q] = jnp.broadcast_to(partial(direction, image), (8, 128))
    gather_start("quad", q, nq, ebuf, e_ss, e_rs)
    for j in range(cz):
        q0[j] = image[j]
    outs[1].start()
    outs[3].start()
    gather_wait("quad", q, nq, ebuf, e_ss, e_rs)
    fbuf[k] = tile_sum(ebuf, nq)
    gather_start("slab", k, ns, fbuf, f_ss, f_rs)
    gather_wait("slab", k, ns, fbuf, f_ss, f_rs)
    last = rz_next / jnp.sum(tile_sum(fbuf, ns)[0:1], axis=1, keepdims=True)
    step_ref[...] = jnp.broadcast_to(last, (1, nx))
    for c in outs:
        c.wait()
    for c in pending:
        c.wait_send()


def solution(mesh):
    ns, nq = mesh.shape["slab"], mesh.shape["quad"]

    def body(right_side, phase_label, density_gain, subdomain, block_factor, coupling):
        cz, cy, nx = right_side.shape
        count = coupling.shape[2]
        field = pltpu.VMEM((cz, cy, nx), F32)
        dma = pltpu.SemaphoreType.DMA
        shape = jax.ShapeDtypeStruct((cz, cy, nx), F32)
        hbm = pl.BlockSpec(memory_space=pltpu.HBM)
        x_part, p_part, r_part, q_part, step = pl.pallas_call(
            functools.partial(kernel, ns, nq),
            out_shape=(shape, shape, shape, shape, jax.ShapeDtypeStruct((1, nx), F32)),
            in_specs=[hbm] * 6,
            out_specs=(hbm,) * 4 + (pl.BlockSpec(memory_space=pltpu.VMEM),),
            scratch_shapes=[
                field, pltpu.VMEM((cz, cy, nx), jnp.int32), field, pltpu.VMEM((cz, cy, nx), jnp.int32),
                pltpu.VMEM(block_factor.shape, F32), pltpu.VMEM(coupling.shape, F32), field, field,
                dma((6,)), dma((4,)),
                pltpu.VMEM((cz + 1, cy, nx), F32), field, field, field, field, field, field, field,
                pltpu.VMEM((cz, 8, cy, nx), BF16), pltpu.VMEM((cz, 8 * cy, nx), BF16),
                field, field, field, field,
                pltpu.VMEM((ns, count, count), F32), pltpu.VMEM((ns, count // 2, 2 * count), F32),
                pltpu.VMEM((2, nq, 8, 128), F32), pltpu.VMEM((2, ns, 8, 128), F32),
                pltpu.VMEM((2, nq, 8, nq * count), F32),
                pltpu.VMEM((nq, 8, 128), F32), pltpu.VMEM((ns, 8, 128), F32),
                pltpu.VMEM((3, 2, cy, nx), F32), pltpu.VMEM((3, 2, cz, nx), F32), pltpu.VMEM((3, 2, cz, nx), F32),
                pltpu.VMEM((2,) + block_factor.shape[1:], F32), pltpu.VMEM((2, cy, nx), jnp.int32),
                pltpu.VMEM((2, cz, nx), jnp.int32), pltpu.VMEM((2, cz, nx), jnp.int32),
                pltpu.VMEM((2, cy, nx), F32), pltpu.VMEM((2, cy, nx), F32), pltpu.VMEM((2 * cz, nx), F32),
                dma((ns,)), dma((ns,)), dma((2, nq)), dma((2, nq)), dma((2, ns)), dma((2, ns)),
                dma((2, nq)), dma((2, nq)), dma((nq,)), dma((nq,)),
                dma((ns,)), dma((ns,)), dma((5, 4)), dma((5, 4)),
            ],
            compiler_params=pltpu.CompilerParams(
                collective_id=0, has_side_effects=True, vmem_limit_bytes=40 * 1024 * 1024),
        )(*(pltpu.with_memory_space_constraint(value, pltpu.HBM) for value in (
            right_side, phase_label, density_gain, subdomain, block_factor, coupling)))
        return x_part + step * p_part, r_part - step * q_part

    spec = P("slab", "quad", None)
    return jax.shard_map(body, mesh=mesh, in_specs=(spec,) * 6, out_specs=(spec, spec), check_vma=False)
```

```python
import functools

import jax
import jax.numpy as jnp
from jax import lax
from jax.experimental import pallas as pl
from jax.experimental.pallas import tpu as pltpu
from jax.sharding import PartitionSpec as P

LINE = 4
ITERS = 2
MESH = pl.DeviceIdType.MESH
F32 = jnp.float32
BF16 = jnp.bfloat16


def kernel(ns, nq, b_hbm, phase_hbm, gain_hbm, sub_hbm, fac_hbm, cpl_hbm, x_out, p_out, r_out, q_out, step_ref,
           b_ref, phase_ref, gain_ref, sub_ref, fac_ref, cpl_ref, x_ref, r_ref, in_sem, out_sem, kz, kyl, kyh, kxl, kxh, diag, inv, gam, hot_hi, hot_lo, p0, q0, bj, zz,
           cg, cgw, qbuf, sbuf, rbuf, ebuf, fbuf, zhalo, yhalo, ysend,
           fach, zsub, ysub, ysend_sub, zp, zq, yp,
           cg_ss, cg_rs, q_ss, q_rs, s_ss, s_rs, r_ss, r_rs, e_ss, e_rs, f_ss, f_rs, h_ss, h_rs):
    k = lax.axis_index("slab")
    q = lax.axis_index("quad")
    cz, cy, nx = b_ref.shape
    count = cpl_ref.shape[2]
    pending = []
    loads = [pltpu.make_async_copy(src, dst, in_sem.at[i]) for i, (src, dst) in enumerate((
        (phase_hbm, phase_ref), (gain_hbm, gain_ref), (cpl_hbm, cpl_ref),
        (sub_hbm, sub_ref), (b_hbm, b_ref), (fac_hbm, fac_ref)))]
    for c in loads:
        c.start()

    barrier = pltpu.get_barrier_semaphore()
    for d in range(1, ns):
        pl.semaphore_signal(barrier, inc=1, device_id={"slab": lax.rem(k + d, ns)}, device_id_type=MESH)
    for d in range(1, nq):
        pl.semaphore_signal(barrier, inc=1, device_id={"quad": lax.rem(q + d, nq)}, device_id_type=MESH)

    def copies(axis, me, n, buf, ss, rs):
        out = []
        for d in range(1, n):
            out.append(pltpu.make_async_remote_copy(
                src_ref=buf.at[me], dst_ref=buf.at[me], send_sem=ss.at[d], recv_sem=rs.at[d],
                device_id={axis: lax.rem(me + d, n)}, device_id_type=MESH))
        return out

    def gather_start(axis, me, n, buf, ss, rs):
        for c in copies(axis, me, n, buf, ss, rs):
            c.start()
            pending.append(c)

    def gather_wait(axis, me, n, buf, ss, rs):
        for d in range(1, n):
            at = lax.rem(me + n - d, n)
            pltpu.make_async_remote_copy(
                src_ref=buf.at[at], dst_ref=buf.at[at], send_sem=ss.at[d], recv_sem=rs.at[d],
                device_id={axis: at}, device_id_type=MESH).wait_recv()

    row = lax.broadcasted_iota(jnp.int32, (cy, nx), 0)
    lane = lax.broadcasted_iota(jnp.int32, (cy, nx), 1)
    sub8 = lax.broadcasted_iota(jnp.int32, (8, 128), 0)
    lane1 = lax.broadcasted_iota(jnp.int32, (1, 128), 1)
    lane8 = lax.broadcasted_iota(jnp.int32, (8, 128), 1)
    eye = (lax.broadcasted_iota(jnp.int32, (count, count), 0)
           == lax.broadcasted_iota(jnp.int32, (count, count), 1)).astype(F32)

    halos = [(zhalo.at[i], yhalo.at[i], ysend.at[i]) for i in range(3)] + [(zsub, ysub, ysend_sub)]

    def halo_parts(slot, src):
        up, down = jnp.minimum(k + 1, ns - 1), jnp.maximum(k - 1, 0)
        right, left = jnp.minimum(q + 1, nq - 1), jnp.maximum(q - 1, 0)

        def copy(s, dst, i, axis, to):
            return pltpu.make_async_remote_copy(
                src_ref=s, dst_ref=dst, send_sem=h_ss.at[slot, i], recv_sem=h_rs.at[slot, i],
                device_id={axis: to}, device_id_type=MESH)

        if slot == 4:
            return ((k < ns - 1, k > 0, copy(src, fach.at[0], 0, "slab", up)),
                    (k > 0, k < ns - 1, copy(src, fach.at[1], 1, "slab", down)))
        zdst, ydst, ysrc = halos[slot]
        return (
            (k < ns - 1, k > 0, copy(src.at[cz - 1], zdst.at[0], 0, "slab", up)),
            (k > 0, k < ns - 1, copy(src.at[0], zdst.at[1], 1, "slab", down)),
            (q < nq - 1, q > 0, copy(ysrc.at[1], ydst.at[0], 2, "quad", right)),
            (q > 0, q < nq - 1, copy(ysrc.at[0], ydst.at[1], 3, "quad", left)),
        )

    def halo_clear():
        for zdst, ydst, unused in halos:
            for buf, i, edge in ((zdst, 0, k == 0), (zdst, 1, k == ns - 1),
                                 (ydst, 0, q == 0), (ydst, 1, q == nq - 1)):
                @pl.when(edge)
                def _(buf=buf, i=i):
                    buf[i] = jnp.zeros(buf.shape[1:], buf.dtype)
        for i, edge in ((0, k == 0), (1, k == ns - 1)):
            @pl.when(edge)
            def _(i=i):
                fach[i] = jnp.zeros(fach.shape[1:], F32)

    def halo_start(slot, src):
        if slot < 4:
            ysrc = halos[slot][2]
            for j in range(cz):
                ysrc[0, j:j + 1] = src[j, 0:1]
                ysrc[1, j:j + 1] = src[j, cy - 1:cy]
        for sends, unused, c in halo_parts(slot, src):
            @pl.when(sends)
            def _(c=c):
                c.start()

    def halo_wait(slot, src):
        for sends, receives, c in halo_parts(slot, src):
            @pl.when(receives)
            def _(c=c):
                c.wait_recv()

            @pl.when(sends)
            def _(c=c):
                c.wait_send()

    def y_below(plane, edge):
        return jnp.where(row == 0, edge, pltpu.roll(plane, 1, 0))

    def y_above(plane, edge):
        return jnp.where(row == cy - 1, edge, pltpu.roll(plane, cy - 1, 0))

    def harmonic(here, there):
        return jnp.where(there > 0, 2.0 * here * there / (here + there), here)

    def restrict(planes):
        total = None
        for j in range(cz):
            high = planes[j].astype(BF16)
            low = (planes[j] - high.astype(F32)).astype(BF16)
            lhs = jnp.concatenate([part * hot_hi[j, h] for part in (high, low) for h in range(8)], axis=0)
            now = lax.dot_general(lhs, hot_lo[j], (((1,), (1,)), ((), ())), preferred_element_type=F32)
            total = now if total is None else total + now
        total = total[:8 * cy] + total[8 * cy:]
        spot = lax.broadcasted_iota(jnp.int32, total.shape, 0) % cy
        across = lax.broadcasted_iota(jnp.int32, total.shape, 1) // 8
        total = jnp.where(spot == across, total, 0.0)
        tile = jnp.concatenate(
            [jnp.sum(total[cy * h:cy * (h + 1)], axis=0, keepdims=True) for h in range(8)], axis=0)
        for shift in (8, 16, 32, 64):
            tile = tile + pltpu.roll(tile, shift, 1)
        return jnp.sum(jnp.where(sub8 == lane8 // 8, tile, 0.0), axis=0, keepdims=True)

    def partial(left, right):
        total = left[0] * right[0]
        for j in range(1, cz):
            total = total + left[j] * right[j]
        total = total[:8] + total[8:]
        tile = total[:, :128]
        for c in range(1, nx // 128):
            tile = tile + total[:, 128 * c:128 * (c + 1)]
        return jnp.sum(tile, axis=0, keepdims=True)

    def solve_lines(planes):
        rho = [planes[0] * inv[0]]
        for j in range(1, LINE):
            rho.append((planes[j] + kz[j] * rho[j - 1]) * inv[j])
        values = [None] * LINE
        values[LINE - 1] = rho[LINE - 1]
        for j in range(LINE - 2, -1, -1):
            values[j] = rho[j] - gam[j] * values[j + 1]
        return values

    def pack(vector, *scalars):
        for i, scalar in enumerate(scalars):
            vector = jnp.where(lane1 == count + i, scalar, vector)
        return vector

    def dot(left, right):
        return jnp.sum(partial(left, right), axis=1, keepdims=True)

    def coarse_rhs(slot):
        rows = [jnp.where(lane1 < count, qbuf[slot, i], 0.0) for i in range(nq)]
        pieces = [rows[2 * i] + pltpu.roll(rows[2 * i + 1], 64, 1) for i in range(nq // 2)]
        whole = jnp.concatenate(pieces, axis=1)
        column = jnp.sum(fac_ref[0] * whole, axis=1, keepdims=True)
        return jnp.sum(jnp.concatenate([eye, jnp.zeros_like(eye)], axis=1) * column, axis=0, keepdims=True)

    def chain(rhs):
        us = [rhs[0][:, :count]]
        sq_row, sq_col = us[0] * us[0], None
        for i in range(1, ns):
            if i % 2:
                now = jnp.sum(cg[i] * us[i - 1] + eye * rhs[i][:, :count], axis=1, keepdims=True)
                sq_col = now * now if sq_col is None else sq_col + now * now
            else:
                now = jnp.sum(cg[i] * us[i - 1], axis=0, keepdims=True) + rhs[i][:, :count]
                sq_row = sq_row + now * now
            us.append(now)
        w = us[ns - 1]
        near_row = [jnp.zeros((1, count), F32)] * 3
        near_col = [jnp.where(k + d == ns - 1, w, 0.0) for d in (-1, 0, 1)]
        for i in range(ns - 1, 0, -1):
            if i % 2:
                w = jnp.sum(cg[i] * w, axis=0, keepdims=True) + us[i - 1]
                near_row = [jnp.where(k + d == i - 1, w, old) for d, old in zip((-1, 0, 1), near_row)]
            else:
                w = jnp.sum(cg[i] * w, axis=1, keepdims=True) + us[i - 1]
                near_col = [jnp.where(k + d == i - 1, w, old) for d, old in zip((-1, 0, 1), near_col)]
        near = [col + jnp.sum(eye * line, axis=1, keepdims=True) for col, line in zip(near_col, near_row)]
        square = jnp.sum(sq_row, axis=1, keepdims=True) + jnp.sum(sq_col, axis=0, keepdims=True)
        factors = (fach[0], fac_ref[0], fach[1])
        shares = [jnp.sum(f * w, axis=0, keepdims=True) for f, w in zip(factors, near)]
        return shares, square

    def pack_shares(shares, scalar):
        return jnp.concatenate(shares + [jnp.broadcast_to(scalar, (1, 128))], axis=1)

    def gather_lanes(wide, index):
        return jnp.concatenate(
            [jnp.take_along_axis(wide, index[:, 128 * c:128 * (c + 1)], axis=1, mode="promise_in_bounds")
             for c in range(nx // 128)], axis=1)

    def interpolate(table, index):
        return gather_lanes(jnp.broadcast_to(table, (cy, 128)), index)

    def coarse_tables(slot):
        total = tile_sum(rbuf.at[slot], nq)

        def pick(at, quarter):
            table = jnp.zeros((1, 128), F32)
            for i in range(nq):
                start = nq * count * at + 128 * (i // 2)
                piece = total[:, start:start + 128]
                table = jnp.where(quarter == i, pltpu.roll(piece, 64, 1) if i % 2 else piece, table)
            return table

        sides = jnp.concatenate(
            [jnp.broadcast_to(pick(1, q - 1), (cz, 128)), jnp.broadcast_to(pick(1, q + 1), (cz, 128))], axis=0)
        return pick(1, q), pick(0, q), pick(2, q), sides, total[:, 3 * nq * count:3 * nq * count + 1]

    def tile_sum(buf, n):
        total = buf[0]
        for i in range(1, n):
            total = total + buf[i]
        return total

    def apply(planes):
        images = []
        for j in range(cz):
            below = planes[j - 1] if j > 0 else zp[0]
            above = planes[j + 1] if j < cz - 1 else zp[1]
            v = planes[j]
            images.append(
                diag[j] * v - kz[j] * below - kz[j + 1] * above
                - kyl[j] * y_below(v, yp[j:j + 1]) - kyh[j] * y_above(v, yp[cz + j:cz + j + 1])
                - kxl[j] * pltpu.roll(v, 1, 1) - kxh[j] * pltpu.roll(v, nx - 1, 1))
        return images

    halo_clear()
    loads[3].wait()
    loads[4].wait()
    for j in range(cz):
        label = sub_ref[j]
        high, low = label >> 3, label & 7
        for h in range(8):
            hot_hi[j, h] = jnp.where(high == h, 1.0, 0.0).astype(BF16)
        digit = lax.broadcasted_iota(jnp.int32, (8, nx), 0)
        hot_lo[j] = jnp.concatenate(
            [jnp.where(low[y:y + 1] == digit, 1.0, 0.0) for y in range(cy)], axis=0).astype(BF16)
    right_side = [b_ref[j] for j in range(cz)]
    qbuf[0, q] = restrict(right_side)
    pl.semaphore_wait(barrier, ns - 1 + nq - 1)
    gather_start("quad", q, nq, qbuf.at[0], q_ss.at[0], q_rs.at[0])
    loads[0].wait()
    loads[1].wait()
    for j in range(cz):
        zz[j] = 1.0 / (gain_ref[j] * (0.001 + 0.999 * phase_ref[j].astype(F32)))
    halo_start(0, zz)
    loads[2].wait()
    couple = cpl_ref[0]
    couple = jnp.where(k % 2 == 1, couple, couple.T)
    cgw[k] = jnp.concatenate([couple[:count // 2], couple[count // 2:]], axis=1)
    gather_start("slab", k, ns, cgw, cg_ss, cg_rs)

    m = [zz[j] for j in range(cz)]
    kx_lo = []
    for j in range(cz):
        lo = jnp.where(lane == 0, m[j], harmonic(m[j], pltpu.roll(m[j], 1, 1)))
        hi = jnp.where(lane == nx - 1, m[j], pltpu.roll(lo, nx - 1, 1))
        kx_lo.append(lo + hi)
        kxl[j] = jnp.where(lane == 0, 0.0, lo)
        kxh[j] = jnp.where(lane == nx - 1, 0.0, hi)
    loads[5].wait()
    gather_wait("quad", q, nq, qbuf.at[0], q_ss.at[0], q_rs.at[0])
    sbuf[0, k] = coarse_rhs(0)
    gather_start("slab", k, ns, sbuf.at[0], s_ss.at[0], s_rs.at[0])
    halo_start(4, fac_ref.at[0])
    halo_start(3, sub_ref)
    halo_wait(0, zz)
    kz[0] = harmonic(m[0], zhalo[0, 0])
    for j in range(1, cz):
        kz[j] = harmonic(m[j - 1], m[j])
    kz[cz] = harmonic(m[cz - 1], zhalo[0, 1])
    for j in range(cz):
        lo = harmonic(m[j], y_below(m[j], yhalo[0, 0, j:j + 1]))
        last = harmonic(m[j][cy - 1:cy], yhalo[0, 1, j:j + 1])
        hi = jnp.where(row == cy - 1, last, pltpu.roll(lo, cy - 1, 0))
        kyl[j] = lo
        kyh[j] = hi
        diag[j] = kz[j] + kz[j + 1] + lo + hi + kx_lo[j]
    previous = None
    for j in range(LINE):
        denom = diag[j] if j == 0 else diag[j] + kz[j] * previous
        inverse = 1.0 / denom
        inv[j] = inverse
        if j < LINE - 1:
            previous = -kz[j + 1] * inverse
            gam[j] = previous

    block = solve_lines(right_side)
    for j in range(cz):
        bj[j] = block[j]
    halo_start(1, bj)
    first_dot = dot(right_side, block)
    gather_wait("slab", k, ns, cgw, cg_ss, cg_rs)
    for i in range(ns):
        cg[i, :count // 2] = cgw[i, :, :count]
        cg[i, count // 2:] = cgw[i, :, count:]
    halo_wait(4, fac_ref.at[0])
    gather_wait("slab", k, ns, sbuf.at[0], s_ss.at[0], s_rs.at[0])
    rhs_first = [sbuf[0, i] for i in range(ns)]
    shares, square = chain(rhs_first)
    rbuf[0, q] = pack_shares(shares, square)
    gather_start("quad", q, nq, rbuf.at[0], r_ss.at[0], r_rs.at[0])
    halo_wait(1, bj)
    halo_wait(3, sub_ref)
    ysub_all = jnp.concatenate([ysub[0], ysub[1]], axis=0)
    gather_wait("quad", q, nq, rbuf.at[0], r_ss.at[0], r_rs.at[0])
    table, before, after, sides, first_square = coarse_tables(0)
    for j in range(cz):
        p0[j] = bj[j] + interpolate(table, sub_ref[j])
    zp[0] = zhalo[1, 0] + interpolate(before, zsub[0])
    zp[1] = zhalo[1, 1] + interpolate(after, zsub[1])
    zq[0] = zp[0]
    zq[1] = zp[1]
    yp[...] = jnp.concatenate([yhalo[1, 0], yhalo[1, 1]], axis=0) + gather_lanes(sides, ysub_all)
    direction = [p0[j] for j in range(cz)]
    image = apply(direction)
    for j in range(cz):
        q0[j] = image[j]

    qbuf[1, q] = pack(restrict(image), dot(direction, image), first_dot)
    gather_start("quad", q, nq, qbuf.at[1], q_ss.at[1], q_rs.at[1])
    image = [q0[j] for j in range(cz)]
    image_block = solve_lines(image)
    for j in range(cz):
        zz[j] = image_block[j]
    halo_start(2, zz)
    cross, own_dot = dot(image, [bj[j] for j in range(cz)]), dot(image, image_block)
    gather_wait("quad", q, nq, qbuf.at[1], q_ss.at[1], q_rs.at[1])
    quad_sum = tile_sum(qbuf.at[1], nq)
    sbuf[1, k] = pack(coarse_rhs(1), quad_sum[:, count:count + 1], quad_sum[:, count + 1:count + 2], cross, own_dot)
    gather_start("slab", k, ns, sbuf.at[1], s_ss.at[1], s_rs.at[1])
    gather_wait("slab", k, ns, sbuf.at[1], s_ss.at[1], s_rs.at[1])
    total = tile_sum(sbuf.at[1], ns)
    sums = [total[:, count + i:count + i + 1] for i in range(4)]
    first_dot = sums[1]
    rz = first_dot + first_square
    alpha = rz / sums[0]
    shares, square = chain([sbuf[0, i] - alpha * sbuf[1, i] for i in range(ns)])
    rbuf[1, q] = pack_shares(shares, square - 2.0 * alpha * sums[2] + alpha * alpha * sums[3])
    gather_start("quad", q, nq, rbuf.at[1], r_ss.at[1], r_rs.at[1])
    for j in range(cz):
        r_ref[j] = b_ref[j] - alpha * q0[j]
        x_ref[j] = alpha * p0[j]
        bj[j] = bj[j] - alpha * zz[j]
    outs = [pltpu.make_async_copy(src, dst, out_sem.at[i]) for i, (src, dst) in enumerate((
        (x_ref, x_out), (zz, p_out), (r_ref, r_out), (q0, q_out)))]
    outs[0].start()
    outs[2].start()
    halo_wait(2, zz)
    for i in range(2):
        zp[i] = zhalo[1, i] - alpha * zhalo[2, i]
    yedge = [yhalo[1, i] - alpha * yhalo[2, i] for i in range(2)]
    gather_wait("quad", q, nq, rbuf.at[1], r_ss.at[1], r_rs.at[1])
    table, before, after, sides, last_square = coarse_tables(1)
    rz_next = first_dot + last_square
    beta = rz_next / rz
    for j in range(cz):
        zz[j] = bj[j] + interpolate(table, sub_ref[j]) + beta * p0[j]
    zp[0] = zp[0] + interpolate(before, zsub[0]) + beta * zq[0]
    zp[1] = zp[1] + interpolate(after, zsub[1]) + beta * zq[1]
    yp[...] = jnp.concatenate(yedge, axis=0) + gather_lanes(sides, ysub_all) + beta * yp[...]
    direction = [zz[j] for j in range(cz)]
    image = apply(direction)
    ebuf[q] = partial(direction, image)
    gather_start("quad", q, nq, ebuf, e_ss, e_rs)
    for j in range(cz):
        q0[j] = image[j]
    outs[1].start()
    outs[3].start()
    gather_wait("quad", q, nq, ebuf, e_ss, e_rs)
    fbuf[k] = tile_sum(ebuf, nq)
    gather_start("slab", k, ns, fbuf, f_ss, f_rs)
    gather_wait("slab", k, ns, fbuf, f_ss, f_rs)
    last = rz_next / jnp.sum(tile_sum(fbuf, ns), axis=1, keepdims=True)
    step_ref[...] = jnp.broadcast_to(last, (1, nx))
    for c in outs:
        c.wait()
    for c in pending:
        c.wait_send()


def solution(mesh):
    ns, nq = mesh.shape["slab"], mesh.shape["quad"]

    def body(right_side, phase_label, density_gain, subdomain, block_factor, coupling):
        cz, cy, nx = right_side.shape
        count = coupling.shape[2]
        field = pltpu.VMEM((cz, cy, nx), F32)
        dma = pltpu.SemaphoreType.DMA
        shape = jax.ShapeDtypeStruct((cz, cy, nx), F32)
        hbm = pl.BlockSpec(memory_space=pltpu.HBM)
        x_part, p_part, r_part, q_part, step = pl.pallas_call(
            functools.partial(kernel, ns, nq),
            out_shape=(shape, shape, shape, shape, jax.ShapeDtypeStruct((1, nx), F32)),
            in_specs=[hbm] * 6,
            out_specs=(hbm,) * 4 + (pl.BlockSpec(memory_space=pltpu.VMEM),),
            scratch_shapes=[
                field, pltpu.VMEM((cz, cy, nx), jnp.int32), field, pltpu.VMEM((cz, cy, nx), jnp.int32),
                pltpu.VMEM(block_factor.shape, F32), pltpu.VMEM(coupling.shape, F32), field, field,
                dma((6,)), dma((4,)),
                pltpu.VMEM((cz + 1, cy, nx), F32), field, field, field, field, field, field, field,
                pltpu.VMEM((cz, 8, cy, nx), BF16), pltpu.VMEM((cz, 8 * cy, nx), BF16),
                field, field, field, field,
                pltpu.VMEM((ns, count, count), F32), pltpu.VMEM((ns, count // 2, 2 * count), F32),
                pltpu.VMEM((2, nq, 1, 128), F32), pltpu.VMEM((2, ns, 1, 128), F32),
                pltpu.VMEM((2, nq, 1, 3 * nq * count + 128), F32),
                pltpu.VMEM((nq, 1, 128), F32), pltpu.VMEM((ns, 1, 128), F32),
                pltpu.VMEM((3, 2, cy, nx), F32), pltpu.VMEM((3, 2, cz, nx), F32), pltpu.VMEM((3, 2, cz, nx), F32),
                pltpu.VMEM((2,) + block_factor.shape[1:], F32), pltpu.VMEM((2, cy, nx), jnp.int32),
                pltpu.VMEM((2, cz, nx), jnp.int32), pltpu.VMEM((2, cz, nx), jnp.int32),
                pltpu.VMEM((2, cy, nx), F32), pltpu.VMEM((2, cy, nx), F32), pltpu.VMEM((2 * cz, nx), F32),
                dma((ns,)), dma((ns,)), dma((2, nq)), dma((2, nq)), dma((2, ns)), dma((2, ns)),
                dma((2, nq)), dma((2, nq)), dma((nq,)), dma((nq,)),
                dma((ns,)), dma((ns,)), dma((5, 4)), dma((5, 4)),
            ],
            compiler_params=pltpu.CompilerParams(
                collective_id=0, has_side_effects=True, vmem_limit_bytes=40 * 1024 * 1024),
        )(*(pltpu.with_memory_space_constraint(value, pltpu.HBM) for value in (
            right_side, phase_label, density_gain, subdomain, block_factor, coupling)))
        return x_part + step * p_part, r_part - step * q_part

    spec = P("slab", "quad", None)
    return jax.shard_map(body, mesh=mesh, in_specs=(spec,) * 6, out_specs=(spec, spec), check_vma=False)
```

```python
import functools

import jax
import jax.numpy as jnp
from jax import lax
from jax.experimental import pallas as pl
from jax.experimental.pallas import tpu as pltpu
from jax.sharding import PartitionSpec as P

LINE = 4
ITERS = 2
MESH = pl.DeviceIdType.MESH
F32 = jnp.float32
BF16 = jnp.bfloat16


def kernel(ns, nq, b_hbm, phase_hbm, gain_hbm, sub_hbm, fac_hbm, cpl_hbm, x_out, p_out, r_out, q_out, step_ref,
           b_ref, phase_ref, gain_ref, sub_ref, fac_ref, cpl_ref, x_ref, r_ref, in_sem, out_sem, kz, kyl, kyh, kxl, kxh, diag, inv, gam, hot_hi, hot_lo, p0, q0, bj, zz,
           cg, cgw, qbuf, sbuf, rbuf, ebuf, fbuf, zhalo, yhalo, ysend,
           fach, zsub, ysub, ysend_sub, zp, zq, yp,
           cg_ss, cg_rs, q_ss, q_rs, s_ss, s_rs, r_ss, r_rs, e_ss, e_rs, f_ss, f_rs, h_ss, h_rs):
    k = lax.axis_index("slab")
    q = lax.axis_index("quad")
    cz, cy, nx = b_ref.shape
    count = cpl_ref.shape[2]
    pending = []
    loads = [pltpu.make_async_copy(src, dst, in_sem.at[i]) for i, (src, dst) in enumerate((
        (phase_hbm, phase_ref), (gain_hbm, gain_ref), (cpl_hbm, cpl_ref),
        (sub_hbm, sub_ref), (b_hbm, b_ref), (fac_hbm, fac_ref)))]
    for c in loads:
        c.start()

    barrier = pltpu.get_barrier_semaphore()
    for d in range(1, ns):
        pl.semaphore_signal(barrier, inc=1, device_id={"slab": lax.rem(k + d, ns)}, device_id_type=MESH)
    for d in range(1, nq):
        pl.semaphore_signal(barrier, inc=1, device_id={"quad": lax.rem(q + d, nq)}, device_id_type=MESH)

    def copies(axis, me, n, buf, ss, rs):
        out = []
        for d in range(1, n):
            out.append(pltpu.make_async_remote_copy(
                src_ref=buf.at[me], dst_ref=buf.at[me], send_sem=ss.at[d], recv_sem=rs.at[d],
                device_id={axis: lax.rem(me + d, n)}, device_id_type=MESH))
        return out

    def gather_start(axis, me, n, buf, ss, rs):
        for c in copies(axis, me, n, buf, ss, rs):
            c.start()
            pending.append(c)

    def gather_wait(axis, me, n, buf, ss, rs):
        for d in range(1, n):
            at = lax.rem(me + n - d, n)
            pltpu.make_async_remote_copy(
                src_ref=buf.at[at], dst_ref=buf.at[at], send_sem=ss.at[d], recv_sem=rs.at[d],
                device_id={axis: at}, device_id_type=MESH).wait_recv()

    row = lax.broadcasted_iota(jnp.int32, (cy, nx), 0)
    lane = lax.broadcasted_iota(jnp.int32, (cy, nx), 1)
    sub8 = lax.broadcasted_iota(jnp.int32, (8, 128), 0)
    lane1 = lax.broadcasted_iota(jnp.int32, (1, 128), 1)
    lane8 = lax.broadcasted_iota(jnp.int32, (8, 128), 1)
    eye = (lax.broadcasted_iota(jnp.int32, (count, count), 0)
           == lax.broadcasted_iota(jnp.int32, (count, count), 1)).astype(F32)

    halos = [(zhalo.at[i], yhalo.at[i], ysend.at[i]) for i in range(3)] + [(zsub, ysub, ysend_sub)]

    def halo_parts(slot, src):
        up, down = jnp.minimum(k + 1, ns - 1), jnp.maximum(k - 1, 0)
        right, left = jnp.minimum(q + 1, nq - 1), jnp.maximum(q - 1, 0)

        def copy(s, dst, i, axis, to):
            return pltpu.make_async_remote_copy(
                src_ref=s, dst_ref=dst, send_sem=h_ss.at[slot, i], recv_sem=h_rs.at[slot, i],
                device_id={axis: to}, device_id_type=MESH)

        if slot == 4:
            return ((k < ns - 1, k > 0, copy(src, fach.at[0], 0, "slab", up)),
                    (k > 0, k < ns - 1, copy(src, fach.at[1], 1, "slab", down)))
        zdst, ydst, ysrc = halos[slot]
        return (
            (k < ns - 1, k > 0, copy(src.at[cz - 1], zdst.at[0], 0, "slab", up)),
            (k > 0, k < ns - 1, copy(src.at[0], zdst.at[1], 1, "slab", down)),
            (q < nq - 1, q > 0, copy(ysrc.at[1], ydst.at[0], 2, "quad", right)),
            (q > 0, q < nq - 1, copy(ysrc.at[0], ydst.at[1], 3, "quad", left)),
        )

    def halo_clear():
        for zdst, ydst, unused in halos:
            for buf, i, edge in ((zdst, 0, k == 0), (zdst, 1, k == ns - 1),
                                 (ydst, 0, q == 0), (ydst, 1, q == nq - 1)):
                @pl.when(edge)
                def _(buf=buf, i=i):
                    buf[i] = jnp.zeros(buf.shape[1:], buf.dtype)
        for i, edge in ((0, k == 0), (1, k == ns - 1)):
            @pl.when(edge)
            def _(i=i):
                fach[i] = jnp.zeros(fach.shape[1:], F32)

    def halo_start(slot, src):
        if slot < 4:
            ysrc = halos[slot][2]
            for j in range(cz):
                ysrc[0, j:j + 1] = src[j, 0:1]
                ysrc[1, j:j + 1] = src[j, cy - 1:cy]
        for sends, unused, c in halo_parts(slot, src):
            @pl.when(sends)
            def _(c=c):
                c.start()

    def halo_wait(slot, src):
        for sends, receives, c in halo_parts(slot, src):
            @pl.when(receives)
            def _(c=c):
                c.wait_recv()

            @pl.when(sends)
            def _(c=c):
                c.wait_send()

    def y_below(plane, edge):
        return jnp.where(row == 0, edge, pltpu.roll(plane, 1, 0))

    def y_above(plane, edge):
        return jnp.where(row == cy - 1, edge, pltpu.roll(plane, cy - 1, 0))

    def harmonic(here, there):
        return jnp.where(there > 0, 2.0 * here * there / (here + there), here)

    def restrict(planes):
        total = None
        for j in range(cz):
            high = planes[j].astype(BF16)
            low = (planes[j] - high.astype(F32)).astype(BF16)
            lhs = jnp.concatenate([part * hot_hi[j, h] for part in (high, low) for h in range(8)], axis=0)
            now = lax.dot_general(lhs, hot_lo[j], (((1,), (1,)), ((), ())), preferred_element_type=F32)
            total = now if total is None else total + now
        total = total[:8 * cy] + total[8 * cy:]
        spot = lax.broadcasted_iota(jnp.int32, total.shape, 0) % cy
        across = lax.broadcasted_iota(jnp.int32, total.shape, 1) // 8
        total = jnp.where(spot == across, total, 0.0)
        tile = jnp.concatenate(
            [jnp.sum(total[cy * h:cy * (h + 1)], axis=0, keepdims=True) for h in range(8)], axis=0)
        for shift in (8, 16, 32, 64):
            tile = tile + pltpu.roll(tile, shift, 1)
        return jnp.sum(jnp.where(sub8 == lane8 // 8, tile, 0.0), axis=0, keepdims=True)

    def partial(left, right):
        total = left[0] * right[0]
        for j in range(1, cz):
            total = total + left[j] * right[j]
        total = total[:8] + total[8:]
        tile = total[:, :128]
        for c in range(1, nx // 128):
            tile = tile + total[:, 128 * c:128 * (c + 1)]
        return jnp.sum(tile, axis=0, keepdims=True)

    def solve_lines(planes):
        rho = [planes[0] * inv[0]]
        for j in range(1, LINE):
            rho.append((planes[j] + kz[j] * rho[j - 1]) * inv[j])
        values = [None] * LINE
        values[LINE - 1] = rho[LINE - 1]
        for j in range(LINE - 2, -1, -1):
            values[j] = rho[j] - gam[j] * values[j + 1]
        return values

    def pack(vector, *scalars):
        for i, scalar in enumerate(scalars):
            vector = jnp.where(lane1 == count + i, scalar, vector)
        return vector

    def dot(left, right):
        return jnp.sum(partial(left, right), axis=1, keepdims=True)

    def coarse_rhs(slot):
        rows = [jnp.where(lane1 < count, qbuf[slot, i], 0.0) for i in range(nq)]
        pieces = [rows[2 * i] + pltpu.roll(rows[2 * i + 1], 64, 1) for i in range(nq // 2)]
        whole = jnp.concatenate(pieces, axis=1)
        column = jnp.sum(fac_ref[0] * whole, axis=1, keepdims=True)
        return jnp.sum(jnp.concatenate([eye, jnp.zeros_like(eye)], axis=1) * column, axis=0, keepdims=True)

    def chain(rhs):
        us = [rhs[0][:, :count]]
        sq_row, sq_col = us[0] * us[0], None
        for i in range(1, ns):
            if i % 2:
                now = jnp.sum(cg[i] * us[i - 1] + eye * rhs[i][:, :count], axis=1, keepdims=True)
                sq_col = now * now if sq_col is None else sq_col + now * now
            else:
                now = jnp.sum(cg[i] * us[i - 1], axis=0, keepdims=True) + rhs[i][:, :count]
                sq_row = sq_row + now * now
            us.append(now)
        w = us[ns - 1]
        near_row = [jnp.zeros((1, count), F32)] * 3
        near_col = [jnp.where(k + d == ns - 1, w, 0.0) for d in (-1, 0, 1)]
        for i in range(ns - 1, 0, -1):
            if i % 2:
                w = jnp.sum(cg[i] * w, axis=0, keepdims=True) + us[i - 1]
                near_row = [jnp.where(k + d == i - 1, w, old) for d, old in zip((-1, 0, 1), near_row)]
            else:
                w = jnp.sum(cg[i] * w, axis=1, keepdims=True) + us[i - 1]
                near_col = [jnp.where(k + d == i - 1, w, old) for d, old in zip((-1, 0, 1), near_col)]
        near = [col + jnp.sum(eye * line, axis=1, keepdims=True) for col, line in zip(near_col, near_row)]
        square = jnp.sum(sq_row, axis=1, keepdims=True) + jnp.sum(sq_col, axis=0, keepdims=True)
        factors = (fach[0], fac_ref[0], fach[1])
        shares = [jnp.sum(f * w, axis=0, keepdims=True) for f, w in zip(factors, near)]
        return shares, square

    def pack_shares(shares, scalar):
        return jnp.concatenate(shares + [jnp.broadcast_to(scalar, (1, 128))], axis=1)

    def gather_lanes(wide, index):
        return jnp.concatenate(
            [jnp.take_along_axis(wide, index[:, 128 * c:128 * (c + 1)], axis=1, mode="promise_in_bounds")
             for c in range(nx // 128)], axis=1)

    def interpolate(table, index):
        return gather_lanes(jnp.broadcast_to(table, (cy, 128)), index)

    def coarse_tables(slot):
        total = tile_sum(rbuf.at[slot], nq)

        def pick(at, quarter):
            table = jnp.zeros((1, 128), F32)
            for i in range(nq):
                start = nq * count * at + 128 * (i // 2)
                piece = total[:, start:start + 128]
                table = jnp.where(quarter == i, pltpu.roll(piece, 64, 1) if i % 2 else piece, table)
            return table

        sides = jnp.concatenate(
            [jnp.broadcast_to(pick(1, q - 1), (cz, 128)), jnp.broadcast_to(pick(1, q + 1), (cz, 128))], axis=0)
        return pick(1, q), pick(0, q), pick(2, q), sides, total[:, 3 * nq * count:3 * nq * count + 1]

    def tile_sum(buf, n):
        total = buf[0]
        for i in range(1, n):
            total = total + buf[i]
        return total

    def apply(planes):
        images = []
        for j in range(cz):
            below = planes[j - 1] if j > 0 else zp[0]
            above = planes[j + 1] if j < cz - 1 else zp[1]
            v = planes[j]
            images.append(
                diag[j] * v - kz[j] * below - kz[j + 1] * above
                - kyl[j] * y_below(v, yp[j:j + 1]) - kyh[j] * y_above(v, yp[cz + j:cz + j + 1])
                - kxl[j] * pltpu.roll(v, 1, 1) - kxh[j] * pltpu.roll(v, nx - 1, 1))
        return images

    halo_clear()
    loads[0].wait()
    loads[1].wait()
    for j in range(cz):
        zz[j] = 1.0 / (gain_ref[j] * (0.001 + 0.999 * phase_ref[j].astype(F32)))
    loads[3].wait()
    pl.semaphore_wait(barrier, ns - 1 + nq - 1)
    halo_start(0, zz)
    loads[2].wait()
    couple = cpl_ref[0]
    couple = jnp.where(k % 2 == 1, couple, couple.T)
    cgw[k] = jnp.concatenate([couple[:count // 2], couple[count // 2:]], axis=1)
    gather_start("slab", k, ns, cgw, cg_ss, cg_rs)
    halo_start(3, sub_ref)
    loads[4].wait()
    for j in range(cz):
        label = sub_ref[j]
        high, low = label >> 3, label & 7
        for h in range(8):
            hot_hi[j, h] = jnp.where(high == h, 1.0, 0.0).astype(BF16)
        digit = lax.broadcasted_iota(jnp.int32, (8, nx), 0)
        hot_lo[j] = jnp.concatenate(
            [jnp.where(low[y:y + 1] == digit, 1.0, 0.0) for y in range(cy)], axis=0).astype(BF16)
    right_side = [b_ref[j] for j in range(cz)]
    qbuf[0, q] = restrict(right_side)
    gather_start("quad", q, nq, qbuf.at[0], q_ss.at[0], q_rs.at[0])

    m = [zz[j] for j in range(cz)]
    kx_lo = []
    for j in range(cz):
        lo = jnp.where(lane == 0, m[j], harmonic(m[j], pltpu.roll(m[j], 1, 1)))
        hi = jnp.where(lane == nx - 1, m[j], pltpu.roll(lo, nx - 1, 1))
        kx_lo.append(lo + hi)
        kxl[j] = jnp.where(lane == 0, 0.0, lo)
        kxh[j] = jnp.where(lane == nx - 1, 0.0, hi)
    loads[5].wait()
    gather_wait("quad", q, nq, qbuf.at[0], q_ss.at[0], q_rs.at[0])
    sbuf[0, k] = coarse_rhs(0)
    gather_start("slab", k, ns, sbuf.at[0], s_ss.at[0], s_rs.at[0])
    halo_start(4, fac_ref.at[0])
    halo_wait(0, zz)
    kz[0] = harmonic(m[0], zhalo[0, 0])
    for j in range(1, cz):
        kz[j] = harmonic(m[j - 1], m[j])
    kz[cz] = harmonic(m[cz - 1], zhalo[0, 1])
    for j in range(cz):
        lo = harmonic(m[j], y_below(m[j], yhalo[0, 0, j:j + 1]))
        last = harmonic(m[j][cy - 1:cy], yhalo[0, 1, j:j + 1])
        hi = jnp.where(row == cy - 1, last, pltpu.roll(lo, cy - 1, 0))
        kyl[j] = lo
        kyh[j] = hi
        diag[j] = kz[j] + kz[j + 1] + lo + hi + kx_lo[j]
    previous = None
    for j in range(LINE):
        denom = diag[j] if j == 0 else diag[j] + kz[j] * previous
        inverse = 1.0 / denom
        inv[j] = inverse
        if j < LINE - 1:
            previous = -kz[j + 1] * inverse
            gam[j] = previous

    block = solve_lines(right_side)
    for j in range(cz):
        bj[j] = block[j]
    halo_start(1, bj)
    first_dot = dot(right_side, block)
    gather_wait("slab", k, ns, cgw, cg_ss, cg_rs)
    for i in range(ns):
        cg[i, :count // 2] = cgw[i, :, :count]
        cg[i, count // 2:] = cgw[i, :, count:]
    halo_wait(4, fac_ref.at[0])
    gather_wait("slab", k, ns, sbuf.at[0], s_ss.at[0], s_rs.at[0])
    rhs_first = [sbuf[0, i] for i in range(ns)]
    shares, square = chain(rhs_first)
    rbuf[0, q] = pack_shares(shares, square)
    gather_start("quad", q, nq, rbuf.at[0], r_ss.at[0], r_rs.at[0])
    halo_wait(1, bj)
    halo_wait(3, sub_ref)
    ysub_all = jnp.concatenate([ysub[0], ysub[1]], axis=0)
    gather_wait("quad", q, nq, rbuf.at[0], r_ss.at[0], r_rs.at[0])
    table, before, after, sides, first_square = coarse_tables(0)
    for j in range(cz):
        p0[j] = bj[j] + interpolate(table, sub_ref[j])
    zp[0] = zhalo[1, 0] + interpolate(before, zsub[0])
    zp[1] = zhalo[1, 1] + interpolate(after, zsub[1])
    zq[0] = zp[0]
    zq[1] = zp[1]
    yp[...] = jnp.concatenate([yhalo[1, 0], yhalo[1, 1]], axis=0) + gather_lanes(sides, ysub_all)
    direction = [p0[j] for j in range(cz)]
    image = apply(direction)
    for j in range(cz):
        q0[j] = image[j]

    qbuf[1, q] = pack(restrict(image), dot(direction, image), first_dot)
    gather_start("quad", q, nq, qbuf.at[1], q_ss.at[1], q_rs.at[1])
    image = [q0[j] for j in range(cz)]
    image_block = solve_lines(image)
    for j in range(cz):
        zz[j] = image_block[j]
    halo_start(2, zz)
    cross, own_dot = dot(image, [bj[j] for j in range(cz)]), dot(image, image_block)
    gather_wait("quad", q, nq, qbuf.at[1], q_ss.at[1], q_rs.at[1])
    quad_sum = tile_sum(qbuf.at[1], nq)
    sbuf[1, k] = pack(coarse_rhs(1), quad_sum[:, count:count + 1], quad_sum[:, count + 1:count + 2], cross, own_dot)
    gather_start("slab", k, ns, sbuf.at[1], s_ss.at[1], s_rs.at[1])
    gather_wait("slab", k, ns, sbuf.at[1], s_ss.at[1], s_rs.at[1])
    total = tile_sum(sbuf.at[1], ns)
    sums = [total[:, count + i:count + i + 1] for i in range(4)]
    first_dot = sums[1]
    rz = first_dot + first_square
    alpha = rz / sums[0]
    shares, square = chain([sbuf[0, i] - alpha * sbuf[1, i] for i in range(ns)])
    rbuf[1, q] = pack_shares(shares, square - 2.0 * alpha * sums[2] + alpha * alpha * sums[3])
    gather_start("quad", q, nq, rbuf.at[1], r_ss.at[1], r_rs.at[1])
    for j in range(cz):
        r_ref[j] = b_ref[j] - alpha * q0[j]
        x_ref[j] = alpha * p0[j]
        bj[j] = bj[j] - alpha * zz[j]
    outs = [pltpu.make_async_copy(src, dst, out_sem.at[i]) for i, (src, dst) in enumerate((
        (x_ref, x_out), (zz, p_out), (r_ref, r_out), (q0, q_out)))]
    outs[0].start()
    outs[2].start()
    halo_wait(2, zz)
    for i in range(2):
        zp[i] = zhalo[1, i] - alpha * zhalo[2, i]
    yedge = [yhalo[1, i] - alpha * yhalo[2, i] for i in range(2)]
    gather_wait("quad", q, nq, rbuf.at[1], r_ss.at[1], r_rs.at[1])
    table, before, after, sides, last_square = coarse_tables(1)
    rz_next = first_dot + last_square
    beta = rz_next / rz
    for j in range(cz):
        zz[j] = bj[j] + interpolate(table, sub_ref[j]) + beta * p0[j]
    zp[0] = zp[0] + interpolate(before, zsub[0]) + beta * zq[0]
    zp[1] = zp[1] + interpolate(after, zsub[1]) + beta * zq[1]
    yp[...] = jnp.concatenate(yedge, axis=0) + gather_lanes(sides, ysub_all) + beta * yp[...]
    direction = [zz[j] for j in range(cz)]
    image = apply(direction)
    ebuf[q] = partial(direction, image)
    gather_start("quad", q, nq, ebuf, e_ss, e_rs)
    for j in range(cz):
        q0[j] = image[j]
    outs[1].start()
    outs[3].start()
    gather_wait("quad", q, nq, ebuf, e_ss, e_rs)
    fbuf[k] = tile_sum(ebuf, nq)
    gather_start("slab", k, ns, fbuf, f_ss, f_rs)
    gather_wait("slab", k, ns, fbuf, f_ss, f_rs)
    last = rz_next / jnp.sum(tile_sum(fbuf, ns), axis=1, keepdims=True)
    step_ref[...] = jnp.broadcast_to(last, (1, nx))
    for c in outs:
        c.wait()
    for c in pending:
        c.wait_send()


def solution(mesh):
    ns, nq = mesh.shape["slab"], mesh.shape["quad"]

    def body(right_side, phase_label, density_gain, subdomain, block_factor, coupling):
        cz, cy, nx = right_side.shape
        count = coupling.shape[2]
        field = pltpu.VMEM((cz, cy, nx), F32)
        dma = pltpu.SemaphoreType.DMA
        shape = jax.ShapeDtypeStruct((cz, cy, nx), F32)
        hbm = pl.BlockSpec(memory_space=pltpu.HBM)
        x_part, p_part, r_part, q_part, step = pl.pallas_call(
            functools.partial(kernel, ns, nq),
            out_shape=(shape, shape, shape, shape, jax.ShapeDtypeStruct((1, nx), F32)),
            in_specs=[hbm] * 6,
            out_specs=(hbm,) * 4 + (pl.BlockSpec(memory_space=pltpu.VMEM),),
            scratch_shapes=[
                field, pltpu.VMEM((cz, cy, nx), jnp.int32), field, pltpu.VMEM((cz, cy, nx), jnp.int32),
                pltpu.VMEM(block_factor.shape, F32), pltpu.VMEM(coupling.shape, F32), field, field,
                dma((6,)), dma((4,)),
                pltpu.VMEM((cz + 1, cy, nx), F32), field, field, field, field, field, field, field,
                pltpu.VMEM((cz, 8, cy, nx), BF16), pltpu.VMEM((cz, 8 * cy, nx), BF16),
                field, field, field, field,
                pltpu.VMEM((ns, count, count), F32), pltpu.VMEM((ns, count // 2, 2 * count), F32),
                pltpu.VMEM((2, nq, 1, 128), F32), pltpu.VMEM((2, ns, 1, 128), F32),
                pltpu.VMEM((2, nq, 1, 3 * nq * count + 128), F32),
                pltpu.VMEM((nq, 1, 128), F32), pltpu.VMEM((ns, 1, 128), F32),
                pltpu.VMEM((3, 2, cy, nx), F32), pltpu.VMEM((3, 2, cz, nx), F32), pltpu.VMEM((3, 2, cz, nx), F32),
                pltpu.VMEM((2,) + block_factor.shape[1:], F32), pltpu.VMEM((2, cy, nx), jnp.int32),
                pltpu.VMEM((2, cz, nx), jnp.int32), pltpu.VMEM((2, cz, nx), jnp.int32),
                pltpu.VMEM((2, cy, nx), F32), pltpu.VMEM((2, cy, nx), F32), pltpu.VMEM((2 * cz, nx), F32),
                dma((ns,)), dma((ns,)), dma((2, nq)), dma((2, nq)), dma((2, ns)), dma((2, ns)),
                dma((2, nq)), dma((2, nq)), dma((nq,)), dma((nq,)),
                dma((ns,)), dma((ns,)), dma((5, 4)), dma((5, 4)),
            ],
            compiler_params=pltpu.CompilerParams(
                collective_id=0, has_side_effects=True, vmem_limit_bytes=40 * 1024 * 1024),
        )(*(pltpu.with_memory_space_constraint(value, pltpu.HBM) for value in (
            right_side, phase_label, density_gain, subdomain, block_factor, coupling)))
        return x_part + step * p_part, r_part - step * q_part

    spec = P("slab", "quad", None)
    return jax.shard_map(body, mesh=mesh, in_specs=(spec,) * 6, out_specs=(spec, spec), check_vma=False)
```

```python
import functools

import jax
import jax.numpy as jnp
from jax import lax
from jax.experimental import pallas as pl
from jax.experimental.pallas import tpu as pltpu
from jax.sharding import PartitionSpec as P

LINE = 4
ITERS = 2
MESH = pl.DeviceIdType.MESH
F32 = jnp.float32
BF16 = jnp.bfloat16


def kernel(ns, nq, b_hbm, phase_hbm, gain_hbm, sub_hbm, fac_hbm, cpl_hbm, x_out, p_out, r_out, q_out, step_ref,
           b_ref, phase_ref, gain_ref, sub_ref, fac_ref, cpl_ref, x_ref, r_ref, in_sem, out_sem, kz, kyl, kyh, kxl, kxh, diag, inv, gam, hot_hi, hot_lo, p0, q0, bj, zz,
           cg, cgw, qbuf, sbuf, rbuf, ebuf, fbuf, zhalo, yhalo, ysend,
           fach, zsub, ysub, ysend_sub, zp, zq, yp,
           cg_ss, cg_rs, q_ss, q_rs, s_ss, s_rs, r_ss, r_rs, e_ss, e_rs, f_ss, f_rs, h_ss, h_rs):
    k = lax.axis_index("slab")
    q = lax.axis_index("quad")
    cz, cy, nx = b_ref.shape
    count = cpl_ref.shape[2]
    pending = []
    loads = [pltpu.make_async_copy(src, dst, in_sem.at[i]) for i, (src, dst) in enumerate((
        (sub_hbm, sub_ref), (b_hbm, b_ref), (phase_hbm, phase_ref),
        (gain_hbm, gain_ref), (cpl_hbm, cpl_ref), (fac_hbm, fac_ref)))]
    for c in loads:
        c.start()

    barrier = pltpu.get_barrier_semaphore()
    for d in range(1, ns):
        pl.semaphore_signal(barrier, inc=1, device_id={"slab": lax.rem(k + d, ns)}, device_id_type=MESH)
    for d in range(1, nq):
        pl.semaphore_signal(barrier, inc=1, device_id={"quad": lax.rem(q + d, nq)}, device_id_type=MESH)

    def copies(axis, me, n, buf, ss, rs):
        out = []
        for d in range(1, n):
            out.append(pltpu.make_async_remote_copy(
                src_ref=buf.at[me], dst_ref=buf.at[me], send_sem=ss.at[d], recv_sem=rs.at[d],
                device_id={axis: lax.rem(me + d, n)}, device_id_type=MESH))
        return out

    def gather_start(axis, me, n, buf, ss, rs):
        for c in copies(axis, me, n, buf, ss, rs):
            c.start()
            pending.append(c)

    def gather_wait(axis, me, n, buf, ss, rs):
        for d in range(1, n):
            at = lax.rem(me + n - d, n)
            pltpu.make_async_remote_copy(
                src_ref=buf.at[at], dst_ref=buf.at[at], send_sem=ss.at[d], recv_sem=rs.at[d],
                device_id={axis: at}, device_id_type=MESH).wait_recv()

    row = lax.broadcasted_iota(jnp.int32, (cy, nx), 0)
    lane = lax.broadcasted_iota(jnp.int32, (cy, nx), 1)
    sub8 = lax.broadcasted_iota(jnp.int32, (8, 128), 0)
    lane1 = lax.broadcasted_iota(jnp.int32, (1, 128), 1)
    lane8 = lax.broadcasted_iota(jnp.int32, (8, 128), 1)
    eye = (lax.broadcasted_iota(jnp.int32, (count, count), 0)
           == lax.broadcasted_iota(jnp.int32, (count, count), 1)).astype(F32)

    halos = [(zhalo.at[i], yhalo.at[i], ysend.at[i]) for i in range(3)] + [(zsub, ysub, ysend_sub)]

    def halo_parts(slot, src):
        up, down = jnp.minimum(k + 1, ns - 1), jnp.maximum(k - 1, 0)
        right, left = jnp.minimum(q + 1, nq - 1), jnp.maximum(q - 1, 0)

        def copy(s, dst, i, axis, to):
            return pltpu.make_async_remote_copy(
                src_ref=s, dst_ref=dst, send_sem=h_ss.at[slot, i], recv_sem=h_rs.at[slot, i],
                device_id={axis: to}, device_id_type=MESH)

        if slot == 4:
            return ((k < ns - 1, k > 0, copy(src, fach.at[0], 0, "slab", up)),
                    (k > 0, k < ns - 1, copy(src, fach.at[1], 1, "slab", down)))
        zdst, ydst, ysrc = halos[slot]
        return (
            (k < ns - 1, k > 0, copy(src.at[cz - 1], zdst.at[0], 0, "slab", up)),
            (k > 0, k < ns - 1, copy(src.at[0], zdst.at[1], 1, "slab", down)),
            (q < nq - 1, q > 0, copy(ysrc.at[1], ydst.at[0], 2, "quad", right)),
            (q > 0, q < nq - 1, copy(ysrc.at[0], ydst.at[1], 3, "quad", left)),
        )

    def halo_clear():
        for zdst, ydst, unused in halos:
            for buf, i, edge in ((zdst, 0, k == 0), (zdst, 1, k == ns - 1),
                                 (ydst, 0, q == 0), (ydst, 1, q == nq - 1)):
                @pl.when(edge)
                def _(buf=buf, i=i):
                    buf[i] = jnp.zeros(buf.shape[1:], buf.dtype)
        for i, edge in ((0, k == 0), (1, k == ns - 1)):
            @pl.when(edge)
            def _(i=i):
                fach[i] = jnp.zeros(fach.shape[1:], F32)

    def halo_start(slot, src):
        if slot < 4:
            ysrc = halos[slot][2]
            for j in range(cz):
                ysrc[0, j:j + 1] = src[j, 0:1]
                ysrc[1, j:j + 1] = src[j, cy - 1:cy]
        for sends, unused, c in halo_parts(slot, src):
            @pl.when(sends)
            def _(c=c):
                c.start()

    def halo_wait(slot, src):
        for sends, receives, c in halo_parts(slot, src):
            @pl.when(receives)
            def _(c=c):
                c.wait_recv()

            @pl.when(sends)
            def _(c=c):
                c.wait_send()

    def y_below(plane, edge):
        return jnp.where(row == 0, edge, pltpu.roll(plane, 1, 0))

    def y_above(plane, edge):
        return jnp.where(row == cy - 1, edge, pltpu.roll(plane, cy - 1, 0))

    def harmonic(here, there):
        return jnp.where(there > 0, 2.0 * here * there / (here + there), here)

    def restrict(planes):
        total = None
        for j in range(cz):
            high = planes[j].astype(BF16)
            low = (planes[j] - high.astype(F32)).astype(BF16)
            lhs = jnp.concatenate([part * hot_hi[j, h] for part in (high, low) for h in range(8)], axis=0)
            now = lax.dot_general(lhs, hot_lo[j], (((1,), (1,)), ((), ())), preferred_element_type=F32)
            total = now if total is None else total + now
        total = total[:8 * cy] + total[8 * cy:]
        spot = lax.broadcasted_iota(jnp.int32, total.shape, 0) % cy
        across = lax.broadcasted_iota(jnp.int32, total.shape, 1) // 8
        total = jnp.where(spot == across, total, 0.0)
        tile = jnp.concatenate(
            [jnp.sum(total[cy * h:cy * (h + 1)], axis=0, keepdims=True) for h in range(8)], axis=0)
        for shift in (8, 16, 32, 64):
            tile = tile + pltpu.roll(tile, shift, 1)
        return jnp.sum(jnp.where(sub8 == lane8 // 8, tile, 0.0), axis=0, keepdims=True)

    def partial(left, right):
        total = left[0] * right[0]
        for j in range(1, cz):
            total = total + left[j] * right[j]
        total = total[:8] + total[8:]
        tile = total[:, :128]
        for c in range(1, nx // 128):
            tile = tile + total[:, 128 * c:128 * (c + 1)]
        return jnp.sum(tile, axis=0, keepdims=True)

    def solve_lines(planes):
        rho = [planes[0] * inv[0]]
        for j in range(1, LINE):
            rho.append((planes[j] + kz[j] * rho[j - 1]) * inv[j])
        values = [None] * LINE
        values[LINE - 1] = rho[LINE - 1]
        for j in range(LINE - 2, -1, -1):
            values[j] = rho[j] - gam[j] * values[j + 1]
        return values

    def pack(vector, *scalars):
        for i, scalar in enumerate(scalars):
            vector = jnp.where(lane1 == count + i, scalar, vector)
        return vector

    def dot(left, right):
        return jnp.sum(partial(left, right), axis=1, keepdims=True)

    def coarse_rhs(slot):
        rows = [jnp.where(lane1 < count, qbuf[slot, i], 0.0) for i in range(nq)]
        pieces = [rows[2 * i] + pltpu.roll(rows[2 * i + 1], 64, 1) for i in range(nq // 2)]
        whole = jnp.concatenate(pieces, axis=1)
        column = jnp.sum(fac_ref[0] * whole, axis=1, keepdims=True)
        return jnp.sum(jnp.concatenate([eye, jnp.zeros_like(eye)], axis=1) * column, axis=0, keepdims=True)

    def chain(rhs):
        us = [rhs[0][:, :count]]
        sq_row, sq_col = us[0] * us[0], None
        for i in range(1, ns):
            if i % 2:
                now = jnp.sum(cg[i] * us[i - 1] + eye * rhs[i][:, :count], axis=1, keepdims=True)
                sq_col = now * now if sq_col is None else sq_col + now * now
            else:
                now = jnp.sum(cg[i] * us[i - 1], axis=0, keepdims=True) + rhs[i][:, :count]
                sq_row = sq_row + now * now
            us.append(now)
        w = us[ns - 1]
        near_row = [jnp.zeros((1, count), F32)] * 3
        near_col = [jnp.where(k + d == ns - 1, w, 0.0) for d in (-1, 0, 1)]
        for i in range(ns - 1, 0, -1):
            if i % 2:
                w = jnp.sum(cg[i] * w, axis=0, keepdims=True) + us[i - 1]
                near_row = [jnp.where(k + d == i - 1, w, old) for d, old in zip((-1, 0, 1), near_row)]
            else:
                w = jnp.sum(cg[i] * w, axis=1, keepdims=True) + us[i - 1]
                near_col = [jnp.where(k + d == i - 1, w, old) for d, old in zip((-1, 0, 1), near_col)]
        near = [col + jnp.sum(eye * line, axis=1, keepdims=True) for col, line in zip(near_col, near_row)]
        square = jnp.sum(sq_row, axis=1, keepdims=True) + jnp.sum(sq_col, axis=0, keepdims=True)
        factors = (fach[0], fac_ref[0], fach[1])
        shares = [jnp.sum(f * w, axis=0, keepdims=True) for f, w in zip(factors, near)]
        return shares, square

    def pack_shares(shares, scalar):
        return jnp.concatenate(shares + [jnp.broadcast_to(scalar, (1, 128))], axis=1)

    def gather_lanes(wide, index):
        return jnp.concatenate(
            [jnp.take_along_axis(wide, index[:, 128 * c:128 * (c + 1)], axis=1, mode="promise_in_bounds")
             for c in range(nx // 128)], axis=1)

    def interpolate(table, index):
        return gather_lanes(jnp.broadcast_to(table, (cy, 128)), index)

    def coarse_tables(slot):
        total = tile_sum(rbuf.at[slot], nq)

        def pick(at, quarter):
            table = jnp.zeros((1, 128), F32)
            for i in range(nq):
                start = nq * count * at + 128 * (i // 2)
                piece = total[:, start:start + 128]
                table = jnp.where(quarter == i, pltpu.roll(piece, 64, 1) if i % 2 else piece, table)
            return table

        sides = jnp.concatenate(
            [jnp.broadcast_to(pick(1, q - 1), (cz, 128)), jnp.broadcast_to(pick(1, q + 1), (cz, 128))], axis=0)
        return pick(1, q), pick(0, q), pick(2, q), sides, total[:, 3 * nq * count:3 * nq * count + 1]

    def tile_sum(buf, n):
        total = buf[0]
        for i in range(1, n):
            total = total + buf[i]
        return total

    def apply(planes):
        images = []
        for j in range(cz):
            below = planes[j - 1] if j > 0 else zp[0]
            above = planes[j + 1] if j < cz - 1 else zp[1]
            v = planes[j]
            images.append(
                diag[j] * v - kz[j] * below - kz[j + 1] * above
                - kyl[j] * y_below(v, yp[j:j + 1]) - kyh[j] * y_above(v, yp[cz + j:cz + j + 1])
                - kxl[j] * pltpu.roll(v, 1, 1) - kxh[j] * pltpu.roll(v, nx - 1, 1))
        return images

    halo_clear()
    loads[0].wait()
    loads[1].wait()
    for j in range(cz):
        label = sub_ref[j]
        high, low = label >> 3, label & 7
        for h in range(8):
            hot_hi[j, h] = jnp.where(high == h, 1.0, 0.0).astype(BF16)
        digit = lax.broadcasted_iota(jnp.int32, (8, nx), 0)
        hot_lo[j] = jnp.concatenate(
            [jnp.where(low[y:y + 1] == digit, 1.0, 0.0) for y in range(cy)], axis=0).astype(BF16)
    right_side = [b_ref[j] for j in range(cz)]
    qbuf[0, q] = restrict(right_side)
    pl.semaphore_wait(barrier, ns - 1 + nq - 1)
    gather_start("quad", q, nq, qbuf.at[0], q_ss.at[0], q_rs.at[0])
    loads[2].wait()
    loads[3].wait()
    for j in range(cz):
        zz[j] = 1.0 / (gain_ref[j] * (0.001 + 0.999 * phase_ref[j].astype(F32)))
    halo_start(0, zz)
    loads[4].wait()
    couple = cpl_ref[0]
    couple = jnp.where(k % 2 == 1, couple, couple.T)
    cgw[k] = jnp.concatenate([couple[:count // 2], couple[count // 2:]], axis=1)
    gather_start("slab", k, ns, cgw, cg_ss, cg_rs)

    loads[5].wait()
    gather_wait("quad", q, nq, qbuf.at[0], q_ss.at[0], q_rs.at[0])
    sbuf[0, k] = coarse_rhs(0)
    gather_start("slab", k, ns, sbuf.at[0], s_ss.at[0], s_rs.at[0])
    halo_start(4, fac_ref.at[0])
    halo_start(3, sub_ref)
    m = [zz[j] for j in range(cz)]
    kx_lo = []
    for j in range(cz):
        lo = jnp.where(lane == 0, m[j], harmonic(m[j], pltpu.roll(m[j], 1, 1)))
        hi = jnp.where(lane == nx - 1, m[j], pltpu.roll(lo, nx - 1, 1))
        kx_lo.append(lo + hi)
        kxl[j] = jnp.where(lane == 0, 0.0, lo)
        kxh[j] = jnp.where(lane == nx - 1, 0.0, hi)
    halo_wait(0, zz)
    kz[0] = harmonic(m[0], zhalo[0, 0])
    for j in range(1, cz):
        kz[j] = harmonic(m[j - 1], m[j])
    kz[cz] = harmonic(m[cz - 1], zhalo[0, 1])
    for j in range(cz):
        lo = harmonic(m[j], y_below(m[j], yhalo[0, 0, j:j + 1]))
        last = harmonic(m[j][cy - 1:cy], yhalo[0, 1, j:j + 1])
        hi = jnp.where(row == cy - 1, last, pltpu.roll(lo, cy - 1, 0))
        kyl[j] = lo
        kyh[j] = hi
        diag[j] = kz[j] + kz[j + 1] + lo + hi + kx_lo[j]
    previous = None
    for j in range(LINE):
        denom = diag[j] if j == 0 else diag[j] + kz[j] * previous
        inverse = 1.0 / denom
        inv[j] = inverse
        if j < LINE - 1:
            previous = -kz[j + 1] * inverse
            gam[j] = previous

    block = solve_lines(right_side)
    for j in range(cz):
        bj[j] = block[j]
    halo_start(1, bj)
    first_dot = dot(right_side, block)
    gather_wait("slab", k, ns, cgw, cg_ss, cg_rs)
    for i in range(ns):
        cg[i, :count // 2] = cgw[i, :, :count]
        cg[i, count // 2:] = cgw[i, :, count:]
    halo_wait(4, fac_ref.at[0])
    gather_wait("slab", k, ns, sbuf.at[0], s_ss.at[0], s_rs.at[0])
    rhs_first = [sbuf[0, i] for i in range(ns)]
    shares, square = chain(rhs_first)
    rbuf[0, q] = pack_shares(shares, square)
    gather_start("quad", q, nq, rbuf.at[0], r_ss.at[0], r_rs.at[0])
    halo_wait(1, bj)
    halo_wait(3, sub_ref)
    ysub_all = jnp.concatenate([ysub[0], ysub[1]], axis=0)
    gather_wait("quad", q, nq, rbuf.at[0], r_ss.at[0], r_rs.at[0])
    table, before, after, sides, first_square = coarse_tables(0)
    for j in range(cz):
        p0[j] = bj[j] + interpolate(table, sub_ref[j])
    zp[0] = zhalo[1, 0] + interpolate(before, zsub[0])
    zp[1] = zhalo[1, 1] + interpolate(after, zsub[1])
    zq[0] = zp[0]
    zq[1] = zp[1]
    yp[...] = jnp.concatenate([yhalo[1, 0], yhalo[1, 1]], axis=0) + gather_lanes(sides, ysub_all)
    direction = [p0[j] for j in range(cz)]
    image = apply(direction)
    for j in range(cz):
        q0[j] = image[j]

    qbuf[1, q] = pack(restrict(image), dot(direction, image), first_dot)
    gather_start("quad", q, nq, qbuf.at[1], q_ss.at[1], q_rs.at[1])
    image = [q0[j] for j in range(cz)]
    image_block = solve_lines(image)
    for j in range(cz):
        zz[j] = image_block[j]
    halo_start(2, zz)
    cross, own_dot = dot(image, [bj[j] for j in range(cz)]), dot(image, image_block)
    gather_wait("quad", q, nq, qbuf.at[1], q_ss.at[1], q_rs.at[1])
    quad_sum = tile_sum(qbuf.at[1], nq)
    sbuf[1, k] = pack(coarse_rhs(1), quad_sum[:, count:count + 1], quad_sum[:, count + 1:count + 2], cross, own_dot)
    gather_start("slab", k, ns, sbuf.at[1], s_ss.at[1], s_rs.at[1])
    gather_wait("slab", k, ns, sbuf.at[1], s_ss.at[1], s_rs.at[1])
    total = tile_sum(sbuf.at[1], ns)
    sums = [total[:, count + i:count + i + 1] for i in range(4)]
    first_dot = sums[1]
    rz = first_dot + first_square
    alpha = rz / sums[0]
    shares, square = chain([sbuf[0, i] - alpha * sbuf[1, i] for i in range(ns)])
    rbuf[1, q] = pack_shares(shares, square - 2.0 * alpha * sums[2] + alpha * alpha * sums[3])
    gather_start("quad", q, nq, rbuf.at[1], r_ss.at[1], r_rs.at[1])
    for j in range(cz):
        r_ref[j] = b_ref[j] - alpha * q0[j]
        x_ref[j] = alpha * p0[j]
        bj[j] = bj[j] - alpha * zz[j]
    outs = [pltpu.make_async_copy(src, dst, out_sem.at[i]) for i, (src, dst) in enumerate((
        (x_ref, x_out), (zz, p_out), (r_ref, r_out), (q0, q_out)))]
    outs[0].start()
    outs[2].start()
    halo_wait(2, zz)
    for i in range(2):
        zp[i] = zhalo[1, i] - alpha * zhalo[2, i]
    yedge = [yhalo[1, i] - alpha * yhalo[2, i] for i in range(2)]
    gather_wait("quad", q, nq, rbuf.at[1], r_ss.at[1], r_rs.at[1])
    table, before, after, sides, last_square = coarse_tables(1)
    rz_next = first_dot + last_square
    beta = rz_next / rz
    for j in range(cz):
        zz[j] = bj[j] + interpolate(table, sub_ref[j]) + beta * p0[j]
    zp[0] = zp[0] + interpolate(before, zsub[0]) + beta * zq[0]
    zp[1] = zp[1] + interpolate(after, zsub[1]) + beta * zq[1]
    yp[...] = jnp.concatenate(yedge, axis=0) + gather_lanes(sides, ysub_all) + beta * yp[...]
    direction = [zz[j] for j in range(cz)]
    image = apply(direction)
    ebuf[q] = partial(direction, image)
    gather_start("quad", q, nq, ebuf, e_ss, e_rs)
    for j in range(cz):
        q0[j] = image[j]
    outs[1].start()
    outs[3].start()
    gather_wait("quad", q, nq, ebuf, e_ss, e_rs)
    fbuf[k] = tile_sum(ebuf, nq)
    gather_start("slab", k, ns, fbuf, f_ss, f_rs)
    for c in outs:
        c.wait()
    for c in pending:
        c.wait_send()
    gather_wait("slab", k, ns, fbuf, f_ss, f_rs)
    last = rz_next / jnp.sum(tile_sum(fbuf, ns), axis=1, keepdims=True)
    step_ref[...] = jnp.broadcast_to(last, (1, nx))


def solution(mesh):
    ns, nq = mesh.shape["slab"], mesh.shape["quad"]

    def body(right_side, phase_label, density_gain, subdomain, block_factor, coupling):
        cz, cy, nx = right_side.shape
        count = coupling.shape[2]
        field = pltpu.VMEM((cz, cy, nx), F32)
        dma = pltpu.SemaphoreType.DMA
        shape = jax.ShapeDtypeStruct((cz, cy, nx), F32)
        hbm = pl.BlockSpec(memory_space=pltpu.HBM)
        x_part, p_part, r_part, q_part, step = pl.pallas_call(
            functools.partial(kernel, ns, nq),
            out_shape=(shape, shape, shape, shape, jax.ShapeDtypeStruct((1, nx), F32)),
            in_specs=[hbm] * 6,
            out_specs=(hbm,) * 4 + (pl.BlockSpec(memory_space=pltpu.VMEM),),
            scratch_shapes=[
                field, pltpu.VMEM((cz, cy, nx), jnp.int32), field, pltpu.VMEM((cz, cy, nx), jnp.int32),
                pltpu.VMEM(block_factor.shape, F32), pltpu.VMEM(coupling.shape, F32), field, field,
                dma((6,)), dma((4,)),
                pltpu.VMEM((cz + 1, cy, nx), F32), field, field, field, field, field, field, field,
                pltpu.VMEM((cz, 8, cy, nx), BF16), pltpu.VMEM((cz, 8 * cy, nx), BF16),
                field, field, field, field,
                pltpu.VMEM((ns, count, count), F32), pltpu.VMEM((ns, count // 2, 2 * count), F32),
                pltpu.VMEM((2, nq, 1, 128), F32), pltpu.VMEM((2, ns, 1, 128), F32),
                pltpu.VMEM((2, nq, 1, 3 * nq * count + 128), F32),
                pltpu.VMEM((nq, 1, 128), F32), pltpu.VMEM((ns, 1, 128), F32),
                pltpu.VMEM((3, 2, cy, nx), F32), pltpu.VMEM((3, 2, cz, nx), F32), pltpu.VMEM((3, 2, cz, nx), F32),
                pltpu.VMEM((2,) + block_factor.shape[1:], F32), pltpu.VMEM((2, cy, nx), jnp.int32),
                pltpu.VMEM((2, cz, nx), jnp.int32), pltpu.VMEM((2, cz, nx), jnp.int32),
                pltpu.VMEM((2, cy, nx), F32), pltpu.VMEM((2, cy, nx), F32), pltpu.VMEM((2 * cz, nx), F32),
                dma((ns,)), dma((ns,)), dma((2, nq)), dma((2, nq)), dma((2, ns)), dma((2, ns)),
                dma((2, nq)), dma((2, nq)), dma((nq,)), dma((nq,)),
                dma((ns,)), dma((ns,)), dma((5, 4)), dma((5, 4)),
            ],
            compiler_params=pltpu.CompilerParams(
                collective_id=0, has_side_effects=True, vmem_limit_bytes=40 * 1024 * 1024),
        )(*(pltpu.with_memory_space_constraint(value, pltpu.HBM) for value in (
            right_side, phase_label, density_gain, subdomain, block_factor, coupling)))
        return x_part + step * p_part, r_part - step * q_part

    spec = P("slab", "quad", None)
    return jax.shard_map(body, mesh=mesh, in_specs=(spec,) * 6, out_specs=(spec, spec), check_vma=False)
```
